256 devices in a mesh: dp: 32 (over y, x, core), tensor: 8 (over z).
Axes of the slice: x: 4, y: 4, z: 8, core: 2. Of those that a mesh axis runs over, the one named last changes fastest.
Arguments:
- grads: bfloat16 [32, 1024, 12288], P('dp', None, 'tensor'), may hold values from -6 to 6
- errors: bfloat16 [32, 1024, 12288], P('dp', None, 'tensor'), may hold values from -4 to 4
- q_prev: float32 [12288, 64], P('tensor'), may hold values from -6 to 6
Outputs:
- update: bfloat16 [1024, 12288], P('dp', 'tensor')
- q_new: float32 [12288, 64], P('tensor')
- new_errors: bfloat16 [32, 1024, 12288], P('dp', None, 'tensor')
The draws below stay inside these ranges and needn't reach their ends.
All inputs are finite; a program needn't handle non-finite values.
Results may differ from the reference program's by a relative error of at most 0.012.
Values may be sent and summed in bfloat16 or wider, within the bound.
No kernel may reach another device: no remote copies, remote signals or barrier semaphores. Data moves between devices by JAX's collectives and lax.ppermute only.
A program may use at most 64 MiB of HBM per device.

```python
import jax
import jax.numpy as jnp
from jax import lax

ROWS = 1024
COLS = 12288
RANK = 64
REPLICAS = 32
N_DP = 32


def with_spikes(values, own_key, source, target, parts, factor):
    owner, partner = [(jnp.arange(values.shape[dim]) // (values.shape[dim] // parts)).reshape([-1 if axis == dim else 1 for axis in range(values.ndim)]) for dim in (source, target)]
    chosen = jax.random.permutation(own_key, parts)[partner]
    strong = (owner == chosen) | (owner == (partner + parts // 2) % parts)
    return jnp.where(strong, factor * values, values)


def block_scale(rng, dims, split, least, largest):
    factor_of = 1.0
    for position, parts in split:
        draws = jax.random.uniform(jax.random.fold_in(jax.random.fold_in(rng, 6), position), (parts,), jnp.float32, least / len(split), largest / len(split))
        factor_of = factor_of * jnp.repeat(jnp.exp(draws), dims[position] // parts).reshape((-1,) + (1,) * (len(dims) - 1 - position))
    return factor_of


def noise(own_key, shape, spread, reach, cuts=(), kind=jnp.bfloat16):
    result = spread * jax.random.normal(own_key, shape, jnp.float32)
    if cuts:
        result = result * block_scale(own_key, shape, cuts, -0.22, 0.18)
    return jnp.clip(result, -reach, reach).astype(kind)


def heavy_noise(own_key, dims, width, limit, shards, heavy, dtype=jnp.bfloat16):
    result = width * jax.random.normal(own_key, dims, jnp.float32)
    if shards:
        result = result * block_scale(own_key, dims, shards, -0.22, 0.18)
    return jnp.clip(with_spikes(result, jax.random.fold_in(own_key, 3), *heavy), -limit, limit).astype(dtype)


def setup_inputs(seed: int = 0) -> dict:
    seeds = jax.random.split(jax.random.key(seed), 4)
    grads = heavy_noise(seeds[0], (REPLICAS, ROWS, COLS), 1.0, 6.0, ((0, 32), (2, 8)), (0, 1, 32, 2.75))
    errors = noise(seeds[1], (REPLICAS, ROWS, COLS), 0.5, 4.0, ((0, 32), (2, 8)))
    q_prev = noise(seeds[2], (COLS, RANK), 1.0, 6.0, ((0, 8),), jnp.float32)
    return dict(grads=grads, errors=errors, q_prev=q_prev)


def reference(grads, errors, q_prev):
    prior_cast = q_prev.astype(jnp.bfloat16)

    def left_step(total, pair):
        merged = (pair[0].astype(jnp.float32) + pair[1].astype(jnp.float32)).astype(jnp.bfloat16)
        return (total + jnp.dot(merged.astype(jnp.float32), prior_cast.astype(jnp.float32), preferred_element_type=jnp.float32), None)
    left_sum, _ = lax.scan(left_step, jnp.zeros((ROWS, RANK), jnp.float32), (grads, errors))
    left_sum = left_sum / N_DP
    gram_matrix = jnp.dot(left_sum.T, left_sum, precision=lax.Precision.HIGHEST)
    factor = jnp.linalg.cholesky(gram_matrix)
    ortho_left = jax.scipy.linalg.solve_triangular(factor, left_sum.T, lower=True).T.astype(jnp.bfloat16)

    def right_step(total, pair):
        merged = (pair[0].astype(jnp.float32) + pair[1].astype(jnp.float32)).astype(jnp.bfloat16)
        return (total + jnp.dot(merged.T.astype(jnp.float32), ortho_left.astype(jnp.float32), preferred_element_type=jnp.float32), None)
    q_new, _ = lax.scan(right_step, jnp.zeros((COLS, RANK), jnp.float32), (grads, errors))
    q_new = q_new / N_DP
    full_update = jnp.dot(ortho_left.astype(jnp.float32), q_new.astype(jnp.bfloat16).T.astype(jnp.float32), preferred_element_type=jnp.float32)

    def error_step(pair):
        merged = (pair[0].astype(jnp.float32) + pair[1].astype(jnp.float32)).astype(jnp.bfloat16)
        return (merged.astype(jnp.float32) - full_update).astype(jnp.bfloat16)
    new_errors = lax.map(error_step, (grads, errors))
    return (full_update.astype(jnp.bfloat16), q_new, new_errors)
```

```python
import jax
import jax.numpy as jnp
from jax import lax
from jax.sharding import Mesh, PartitionSpec as P

YX = ("y", "x")


def swap_cores(value):
    return lax.ppermute(value, "core", [(0, 1), (1, 0)])


def exchange(value, axes):
    return lax.all_to_all(value, axes, 0, 0)


def spread(value, copies):
    return jnp.broadcast_to(value[None], (copies,) + value.shape)


def per_device(grads, errors, q_prev):
    core = lax.axis_index("core")
    pairs = lax.axis_size("y") * lax.axis_size("x")
    depth = lax.axis_size("z")
    replicas = 2 * pairs
    merged = (grads[0].astype(jnp.float32) + errors[0].astype(jnp.float32)).astype(jnp.bfloat16)
    prior_cast = q_prev.astype(jnp.bfloat16)
    rows, columns = merged.shape
    rank = prior_cast.shape[1]

    def halves(total):
        total = total.reshape(2, -1, *total.shape[1:])
        keep = lax.dynamic_index_in_dim(total, core, 0, keepdims=False)
        give = lax.dynamic_index_in_dim(total, 1 - core, 0, keepdims=False)
        return keep + swap_cores(give)

    def joined(half):
        other = swap_cores(half)
        return jnp.where(core == 0, jnp.concatenate([half, other]), jnp.concatenate([other, half]))

    partial_left = lax.dot_general(
        prior_cast, merged, (((0,), (1,)), ((), ())), preferred_element_type=jnp.float32
    )
    tiles = partial_left.reshape(rank // 16, 16, rows // 128, 128).transpose(0, 2, 1, 3)
    tiles = tiles.reshape(-1, 16, 128)
    mine = jnp.sum(exchange(halves(tiles), YX), axis=0)
    mine = jnp.sum(exchange(spread(mine, depth), "z"), axis=0) / replicas
    left = joined(exchange(spread(mine, pairs), YX))
    left = left.reshape(rank // 16, rows // 128, 16, 128).transpose(0, 2, 1, 3).reshape(rank, rows)

    gram_matrix = lax.dot_general(
        left, left, (((1,), (1,)), ((), ())), precision=lax.Precision.HIGHEST
    )
    factor = jnp.linalg.cholesky(gram_matrix)
    ortho = jax.scipy.linalg.solve_triangular(factor, left, lower=True).astype(jnp.bfloat16)

    partial_right = jnp.dot(ortho, merged, preferred_element_type=jnp.float32)
    wide = rank * columns // (8 * replicas)
    tiles = partial_right.reshape(rank // 8, 8, columns // wide, wide).transpose(0, 2, 1, 3)
    tiles = tiles.reshape(-1, 8, wide)
    mine = jnp.sum(exchange(halves(tiles), YX), axis=0) / replicas
    right = joined(exchange(spread(mine, pairs), YX))
    right = right.reshape(rank // 8, columns // wide, 8, wide).transpose(0, 2, 1, 3)
    right = right.reshape(rank, columns)

    full_update = lax.dot_general(
        ortho, right.astype(jnp.bfloat16), (((0,), (0,)), ((), ())),
        preferred_element_type=jnp.float32,
    )
    new_errors = (merged.astype(jnp.float32) - full_update).astype(jnp.bfloat16)[None]
    row_count = rows // replicas
    row_start = lax.axis_index(("y", "x", "core")) * row_count
    update = lax.dynamic_slice_in_dim(full_update, row_start, row_count, 0).astype(jnp.bfloat16)
    return update, right.T, new_errors


def solution(mesh):
    chips = Mesh(mesh.devices.reshape(4, 4, 2, 8), ("y", "x", "core", "z"))
    dp = ("y", "x", "core")
    placed = (P(dp, None, "z"), P(dp, None, "z"), P("z", None))
    return jax.shard_map(
        per_device,
        mesh=chips,
        in_specs=placed,
        out_specs=(P(dp, "z"), P("z", None), P(dp, None, "z")),
        check_vma=False,
    )
```

```python
import jax
import jax.numpy as jnp
from jax import lax
from jax.experimental import pallas as pl
from jax.experimental.pallas import tpu as pltpu
from jax.sharding import Mesh, PartitionSpec as P

YX = ("y", "x")
VMEM_LIMIT = 48 * 1024 * 1024
WHOLE = pl.BlockSpec(memory_space=pltpu.VMEM)
SCALAR = pl.BlockSpec(memory_space=pltpu.SMEM)
BLOCK_ROWS = 256


def own_first(core, low, high):
    return jnp.where(core == 0, low, high), jnp.where(core == 0, high, low)


def merge_kernel(core_ref, grads_ref, errors_ref, prior_ref, merged_ref, keep_ref, give_ref):
    step = pl.program_id(0)
    merged = (grads_ref[...].astype(jnp.float32) + errors_ref[...].astype(jnp.float32)).astype(
        jnp.bfloat16
    )
    merged_ref[...] = merged
    left = lax.dot_general(
        prior_ref[...].astype(jnp.bfloat16), merged, (((1,), (1,)), ((), ())),
        preferred_element_type=jnp.float32,
    )
    rank, rows = left.shape
    keep, give = own_first(core_ref[0], left[: rank // 2], left[rank // 2 :])
    lanes = rows // 128
    across = keep_ref.shape[0] // (rank // 32)
    for down in range(rank // 32):
        for lane in range(lanes):
            place = down * across + step * lanes + lane
            tile = (slice(16 * down, 16 * down + 16), slice(128 * lane, 128 * lane + 128))
            keep_ref[place] = keep[tile]
            give_ref[place] = give[tile]


def merge(core, grads, errors, prior):
    rows, columns = grads.shape
    rank = prior.shape[0]
    tiles = jax.ShapeDtypeStruct((rows // 128 * (rank // 32), 16, 128), jnp.float32)
    block = pl.BlockSpec((BLOCK_ROWS, columns), lambda i: (i, 0))
    fixed = pl.BlockSpec(tiles.shape, lambda i: (0, 0, 0))
    return pl.pallas_call(
        merge_kernel,
        grid=(rows // BLOCK_ROWS,),
        in_specs=[SCALAR, block, block, pl.BlockSpec(prior.shape, lambda i: (0, 0))],
        out_specs=[block, fixed, fixed],
        out_shape=[jax.ShapeDtypeStruct(grads.shape, jnp.bfloat16), tiles, tiles],
        compiler_params=pltpu.CompilerParams(vmem_limit_bytes=VMEM_LIMIT),
        cost_estimate=pl.CostEstimate(
            flops=2 * rows * columns * rank, bytes_accessed=6 * rows * columns, transcendentals=0
        ),
    )(core, grads, errors, prior)


def inverse_factor(gram):
    rank = gram.shape[0]
    row = lax.broadcasted_iota(jnp.int32, (rank, rank), 0)
    column = lax.broadcasted_iota(jnp.int32, (rank, rank), 1)
    state = jnp.concatenate([gram, jnp.where(row == column, 1.0, 0.0)], axis=1)
    groups = [state[8 * g : 8 * g + 8] for g in range(rank // 8)]
    below = lax.broadcasted_iota(jnp.int32, (8, 2 * rank), 0)
    for k in range(rank):
        own, place = k // 8, k % 8
        pivot_row = groups[own][place : place + 1]
        scale = lax.rsqrt(pivot_row[:, k : k + 1])
        pivot_row = pivot_row * scale
        for g in range(own, rank // 8):
            step = (groups[g][:, k : k + 1] * scale) * pivot_row
            if g > own:
                groups[g] = groups[g] - step
            else:
                groups[g] = jnp.where(
                    below > place, groups[g] - step, jnp.where(below == place, pivot_row, groups[g])
                )
    return jnp.concatenate(groups)[:, rank:]


def ortho_kernel(core_ref, half_ref, other_ref, merged_ref, ortho_ref, keep_ref, give_ref,
                 held_ref, left_ref, sem):
    fetch = pltpu.make_async_copy(merged_ref, held_ref, sem)
    fetch.start()
    core = core_ref[0]
    rank, rows = left_ref.shape
    across = rows // 128
    for place in range(half_ref.shape[0]):
        low, high = own_first(core, half_ref[place], other_ref[place])
        down = 16 * (place // across)
        lane = pl.ds(128 * (place % across), 128)
        left_ref[pl.ds(down, 16), lane] = low
        left_ref[pl.ds(rank // 2 + down, 16), lane] = high
    left = left_ref[...]
    gram = lax.dot_general(
        left, left, (((1,), (1,)), ((), ())), precision=lax.Precision.HIGHEST,
        preferred_element_type=jnp.float32,
    )
    ortho = jnp.dot(
        inverse_factor(gram), left, precision=lax.Precision.HIGHEST,
        preferred_element_type=jnp.float32,
    ).astype(jnp.bfloat16)
    ortho_ref[...] = ortho
    fetch.wait()
    wide = keep_ref.shape[2]
    count = held_ref.shape[1] // wide
    for lane in range(count):
        right = jnp.dot(
            ortho, held_ref[:, wide * lane : wide * lane + wide],
            preferred_element_type=jnp.float32,
        )
        keep, give = own_first(core, right[: rank // 2], right[rank // 2 :])
        for down in range(rank // 16):
            keep_ref[down * count + lane] = keep[8 * down : 8 * down + 8]
            give_ref[down * count + lane] = give[8 * down : 8 * down + 8]


def orthonormal(core, half, other, merged, parts):
    rows, columns = merged.shape
    rank = half.size * 2 // rows
    wide = rank * columns // (8 * parts)
    tiles = jax.ShapeDtypeStruct((parts // 2, 8, wide), jnp.float32)
    return pl.pallas_call(
        ortho_kernel,
        in_specs=[SCALAR, WHOLE, WHOLE, pl.BlockSpec(memory_space=pl.ANY)],
        out_specs=[WHOLE, WHOLE, WHOLE],
        out_shape=[jax.ShapeDtypeStruct((rank, rows), jnp.bfloat16), tiles, tiles],
        scratch_shapes=[
            pltpu.VMEM((rows, columns), jnp.bfloat16),
            pltpu.VMEM((rank, rows), jnp.float32),
            pltpu.SemaphoreType.DMA,
        ],
        compiler_params=pltpu.CompilerParams(vmem_limit_bytes=VMEM_LIMIT),
        cost_estimate=pl.CostEstimate(
            flops=2 * rows * columns * rank, bytes_accessed=2 * rows * columns, transcendentals=0
        ),
    )(core, half, other, merged)


def finish_kernel(core_ref, half_ref, other_ref, ortho_ref, own_ref, merged_ref,
                  update_ref, right_ref, errors_ref, cast_ref):
    rank = ortho_ref.shape[1]

    @pl.when(pl.program_id(0) == 0)
    def _():
        core = core_ref[0]
        wide = half_ref.shape[2]
        count = right_ref.shape[1] // wide
        for lane in range(count):
            pairs = [
                own_first(core, half_ref[down * count + lane], other_ref[down * count + lane])
                for down in range(rank // 16)
            ]
            right = jnp.concatenate([low for low, _ in pairs] + [high for _, high in pairs])
            cast_ref[:, wide * lane : wide * lane + wide] = right.astype(jnp.bfloat16)
            right_ref[:, wide * lane : wide * lane + wide] = right
        update_ref[...] = jnp.dot(
            own_ref[...], cast_ref[...], preferred_element_type=jnp.float32
        ).astype(jnp.bfloat16)

    full_update = jnp.dot(ortho_ref[...], cast_ref[...], preferred_element_type=jnp.float32)
    errors_ref[...] = (merged_ref[...].astype(jnp.float32) - full_update).astype(jnp.bfloat16)


def finish(core, half, other, ortho, own, merged):
    rows, columns = merged.shape
    rank = ortho.shape[1]
    block = pl.BlockSpec((BLOCK_ROWS, columns), lambda i: (i, 0))
    tiles = pl.BlockSpec(half.shape, lambda i: (0, 0, 0))

    def fixed(shape):
        return pl.BlockSpec(shape, lambda i: (0, 0))

    return pl.pallas_call(
        finish_kernel,
        grid=(rows // BLOCK_ROWS,),
        in_specs=[
            SCALAR, tiles, tiles, pl.BlockSpec((BLOCK_ROWS, rank), lambda i: (i, 0)),
            fixed(own.shape), block,
        ],
        out_specs=[fixed((own.shape[0], columns)), fixed((rank, columns)), block],
        out_shape=[
            jax.ShapeDtypeStruct((own.shape[0], columns), jnp.bfloat16),
            jax.ShapeDtypeStruct((rank, columns), jnp.float32),
            jax.ShapeDtypeStruct(merged.shape, jnp.bfloat16),
        ],
        scratch_shapes=[pltpu.VMEM((rank, columns), jnp.bfloat16)],
        compiler_params=pltpu.CompilerParams(vmem_limit_bytes=VMEM_LIMIT),
        cost_estimate=pl.CostEstimate(
            flops=2 * rows * columns * rank, bytes_accessed=4 * rows * columns, transcendentals=0
        ),
    )(core, half, other, ortho, own, merged)


def swap_cores(value):
    return lax.ppermute(value, "core", [(0, 1), (1, 0)])


def exchange(value, axes):
    return lax.all_to_all(value, axes, 0, 0)


def spread(value, copies):
    return jnp.broadcast_to(value[None], (copies,) + value.shape)


def per_device(grads, errors, q_prev):
    core = lax.axis_index("core").astype(jnp.int32).reshape(1)
    pairs = lax.axis_size("y") * lax.axis_size("x")
    depth = lax.axis_size("z")
    replicas = 2 * pairs

    merged, keep, give = merge(core, grads[0], errors[0], q_prev.T)
    mine = jnp.sum(exchange(keep + swap_cores(give), YX), axis=0)
    mine = jnp.sum(exchange(spread(mine, depth), "z"), axis=0) / replicas
    half = exchange(spread(mine, pairs), YX)

    ortho, keep, give = orthonormal(core, half, swap_cores(half), merged, replicas)
    mine = jnp.sum(exchange(keep + swap_cores(give), YX), axis=0) / replicas
    half = exchange(spread(mine, pairs), YX)

    ortho = ortho.T
    row_count = grads.shape[1] // replicas
    row_start = lax.axis_index(("y", "x", "core")) * row_count
    own = lax.dynamic_slice_in_dim(ortho, row_start, row_count, 0)
    update, right, new_errors = finish(core, half, swap_cores(half), ortho, own, merged)
    return update, right.T, new_errors[None]


def solution(mesh):
    chips = Mesh(mesh.devices.reshape(4, 4, 2, 8), ("y", "x", "core", "z"))
    dp = ("y", "x", "core")
    placed = (P(dp, None, "z"), P(dp, None, "z"), P("z", None))
    return jax.shard_map(
        per_device,
        mesh=chips,
        in_specs=placed,
        out_specs=(P(dp, "z"), P("z", None), P(dp, None, "z")),
        check_vma=False,
    )
```

```python
import jax
import jax.numpy as jnp
from jax import lax
from jax.experimental import pallas as pl
from jax.experimental.pallas import tpu as pltpu
from jax.sharding import Mesh, PartitionSpec as P

YX = ("y", "x")
VMEM_LIMIT = 32 * 1024 * 1024
WHOLE = pl.BlockSpec(memory_space=pltpu.VMEM)
SCALAR = pl.BlockSpec(memory_space=pltpu.SMEM)
IN_HBM = pl.BlockSpec(memory_space=pltpu.HBM)
CHUNK = 128
GROUP = 8


def own_first(core, low, high):
    return jnp.where(core == 0, low, high), jnp.where(core == 0, high, low)


def merge_kernel(core_ref, grads_ref, errors_ref, prior_ref, merged_ref, keep_ref, give_ref,
                 grads_held, errors_held, sems):
    core = core_ref[0]
    rank = prior_ref.shape[0]
    rows = merged_ref.shape[0]
    chunks = rows // CHUNK
    fetches = []
    for i in range(chunks):
        block = pl.ds(CHUNK * i, CHUNK)
        pair = (
            pltpu.make_async_copy(grads_ref.at[block], grads_held.at[block], sems.at[0, i]),
            pltpu.make_async_copy(errors_ref.at[block], errors_held.at[block], sems.at[1, i]),
        )
        for fetch in pair:
            fetch.start()
        fetches.append(pair)
    prior = prior_ref[...].astype(jnp.bfloat16)
    for i in range(chunks):
        block = pl.ds(CHUNK * i, CHUNK)
        for fetch in fetches[i]:
            fetch.wait()
        merged = (
            grads_held[block].astype(jnp.float32) + errors_held[block].astype(jnp.float32)
        ).astype(jnp.bfloat16)
        merged_ref[block] = merged
        left = lax.dot_general(
            prior, merged, (((1,), (1,)), ((), ())), preferred_element_type=jnp.float32
        )
        keep, give = own_first(core, left[: rank // 2], left[rank // 2 :])
        for down in range(rank // 32):
            for lane in range(CHUNK // 128):
                place = down * (rows // 128) + i * (CHUNK // 128) + lane
                tile = (slice(16 * down, 16 * down + 16), slice(128 * lane, 128 * lane + 128))
                keep_ref[place] = keep[tile]
                give_ref[place] = give[tile]


def merge(core, grads, errors, prior):
    rows, columns = grads.shape
    rank = prior.shape[0]
    tiles = jax.ShapeDtypeStruct((rows // 128 * (rank // 32), 16, 128), jnp.float32)
    return pl.pallas_call(
        merge_kernel,
        in_specs=[SCALAR, IN_HBM, IN_HBM, WHOLE],
        out_specs=[WHOLE, WHOLE, WHOLE],
        out_shape=[jax.ShapeDtypeStruct(grads.shape, jnp.bfloat16), tiles, tiles],
        scratch_shapes=[
            pltpu.VMEM(grads.shape, jnp.bfloat16),
            pltpu.VMEM(grads.shape, jnp.bfloat16),
            pltpu.SemaphoreType.DMA((2, rows // CHUNK)),
        ],
        compiler_params=pltpu.CompilerParams(vmem_limit_bytes=VMEM_LIMIT),
        cost_estimate=pl.CostEstimate(
            flops=2 * rows * columns * rank, bytes_accessed=6 * rows * columns, transcendentals=0
        ),
    )(core, grads, errors, prior)


def inverse_factor(gram):
    rank = gram.shape[0]
    shape = (GROUP, 2 * rank)
    row = lax.broadcasted_iota(jnp.int32, (rank, rank), 0)
    column = lax.broadcasted_iota(jnp.int32, (rank, rank), 1)
    state = jnp.concatenate([gram, jnp.where(row == column, 1.0, 0.0)], axis=1)
    groups = [state[GROUP * g : GROUP * g + GROUP] for g in range(rank // GROUP)]
    place = lax.broadcasted_iota(jnp.int32, shape, 0)
    span = range(GROUP)
    for own in range(rank // GROUP):
        later = range(own, rank // GROUP)
        first = GROUP * own
        columns = [
            {g: jnp.broadcast_to(groups[g][:, first + j : first + j + 1], shape) for g in later}
            for j in span
        ]
        rows = [jnp.broadcast_to(groups[own][j : j + 1], shape) for j in span]
        cross = [
            [jnp.broadcast_to(columns[j][own][i : i + 1], shape) for j in range(i + 1)] for i in span
        ]
        for j in span:
            scale = lax.rsqrt(cross[j][j])
            rows[j] = rows[j] * scale
            for g in later:
                columns[j][g] = columns[j][g] * scale
            for i in range(j + 1, GROUP):
                cross[i][j] = cross[i][j] * scale
            for i in range(j + 1, GROUP):
                rows[i] = rows[i] - cross[i][j] * rows[j]
                for g in later:
                    columns[i][g] = columns[i][g] - columns[j][g] * cross[i][j]
                for l in range(j + 1, i + 1):
                    cross[i][l] = cross[i][l] - cross[i][j] * cross[l][j]
        for g in range(own + 1, rank // GROUP):
            for j in span:
                groups[g] = groups[g] - columns[j][g] * rows[j]
        groups[own] = rows[0]
        for j in range(1, GROUP):
            groups[own] = jnp.where(place == j, rows[j], groups[own])
    return jnp.concatenate(groups)[:, rank:]


def ortho_kernel(core_ref, half_ref, other_ref, merged_ref, ortho_ref, keep_ref, give_ref,
                 left_ref):
    core = core_ref[0]
    rank, rows = left_ref.shape
    across = rows // 128
    for place in range(half_ref.shape[0]):
        low, high = own_first(core, half_ref[place], other_ref[place])
        down = 16 * (place // across)
        lane = pl.ds(128 * (place % across), 128)
        left_ref[pl.ds(down, 16), lane] = low
        left_ref[pl.ds(rank // 2 + down, 16), lane] = high
    left = left_ref[...]
    gram = lax.dot_general(
        left, left, (((1,), (1,)), ((), ())), precision=lax.Precision.HIGHEST,
        preferred_element_type=jnp.float32,
    )
    ortho = jnp.dot(
        inverse_factor(gram), left, precision=lax.Precision.HIGHEST,
        preferred_element_type=jnp.float32,
    ).astype(jnp.bfloat16)
    ortho_ref[...] = ortho
    wide = keep_ref.shape[2]
    count = merged_ref.shape[1] // wide
    for lane in range(count):
        right = jnp.dot(
            ortho, merged_ref[:, wide * lane : wide * lane + wide],
            preferred_element_type=jnp.float32,
        )
        keep, give = own_first(core, right[: rank // 2], right[rank // 2 :])
        for down in range(rank // 16):
            keep_ref[down * count + lane] = keep[8 * down : 8 * down + 8]
            give_ref[down * count + lane] = give[8 * down : 8 * down + 8]


def orthonormal(core, half, other, merged, parts):
    rows, columns = merged.shape
    rank = half.size * 2 // rows
    wide = rank * columns // (8 * parts)
    tiles = jax.ShapeDtypeStruct((parts // 2, 8, wide), jnp.float32)
    return pl.pallas_call(
        ortho_kernel,
        in_specs=[SCALAR, WHOLE, WHOLE, WHOLE],
        out_specs=[WHOLE, WHOLE, WHOLE],
        out_shape=[jax.ShapeDtypeStruct((rank, rows), jnp.bfloat16), tiles, tiles],
        scratch_shapes=[pltpu.VMEM((rank, rows), jnp.float32)],
        compiler_params=pltpu.CompilerParams(vmem_limit_bytes=VMEM_LIMIT),
        cost_estimate=pl.CostEstimate(
            flops=2 * rows * columns * rank, bytes_accessed=2 * rows * columns, transcendentals=0
        ),
    )(core, half, other, merged)


def finish_kernel(core_ref, half_ref, other_ref, ortho_ref, own_ref, merged_ref,
                  update_ref, right_ref, errors_ref, cast_ref, errors_held, sems):
    core = core_ref[0]
    rank = ortho_ref.shape[1]
    wide = half_ref.shape[2]
    count = right_ref.shape[1] // wide
    for lane in range(count):
        pairs = [
            own_first(core, half_ref[down * count + lane], other_ref[down * count + lane])
            for down in range(rank // 16)
        ]
        right = jnp.concatenate([low for low, _ in pairs] + [high for _, high in pairs])
        cast_ref[:, wide * lane : wide * lane + wide] = right.astype(jnp.bfloat16)
        right_ref[:, wide * lane : wide * lane + wide] = right
    cast = cast_ref[...]
    stores = []
    for i in range(merged_ref.shape[0] // CHUNK):
        block = pl.ds(CHUNK * i, CHUNK)
        full_update = jnp.dot(ortho_ref[block], cast, preferred_element_type=jnp.float32)
        errors_held[block] = (
            merged_ref[block].astype(jnp.float32) - full_update
        ).astype(jnp.bfloat16)
        store = pltpu.make_async_copy(errors_held.at[block], errors_ref.at[block], sems.at[i])
        store.start()
        stores.append(store)
    update_ref[...] = jnp.dot(
        own_ref[...], cast, preferred_element_type=jnp.float32
    ).astype(jnp.bfloat16)
    for store in stores:
        store.wait()


def finish(core, half, other, ortho, own, merged):
    rows, columns = merged.shape
    rank = ortho.shape[1]
    return pl.pallas_call(
        finish_kernel,
        in_specs=[SCALAR, WHOLE, WHOLE, WHOLE, WHOLE, WHOLE],
        out_specs=[WHOLE, WHOLE, IN_HBM],
        out_shape=[
            jax.ShapeDtypeStruct((own.shape[0], columns), jnp.bfloat16),
            jax.ShapeDtypeStruct((rank, columns), jnp.float32),
            jax.ShapeDtypeStruct(merged.shape, jnp.bfloat16),
        ],
        scratch_shapes=[
            pltpu.VMEM((rank, columns), jnp.bfloat16),
            pltpu.VMEM(merged.shape, jnp.bfloat16),
            pltpu.SemaphoreType.DMA((rows // CHUNK,)),
        ],
        compiler_params=pltpu.CompilerParams(vmem_limit_bytes=VMEM_LIMIT),
        cost_estimate=pl.CostEstimate(
            flops=2 * rows * columns * rank, bytes_accessed=4 * rows * columns, transcendentals=0
        ),
    )(core, half, other, ortho, own, merged)


def swap_cores(value):
    return lax.ppermute(value, "core", [(0, 1), (1, 0)])


def exchange(value, axes):
    return lax.all_to_all(value, axes, 0, 0)


def spread(value, copies):
    return jnp.broadcast_to(value[None], (copies,) + value.shape)


def per_device(grads, errors, q_prev):
    core = lax.axis_index("core").astype(jnp.int32).reshape(1)
    pairs = lax.axis_size("y") * lax.axis_size("x")
    depth = lax.axis_size("z")
    replicas = 2 * pairs

    merged, keep, give = merge(core, grads[0], errors[0], q_prev.T)
    mine = jnp.sum(exchange(keep + swap_cores(give), YX), axis=0)
    mine = jnp.sum(exchange(spread(mine, depth), "z"), axis=0) / replicas
    half = exchange(spread(mine, pairs), YX)

    ortho, keep, give = orthonormal(core, half, swap_cores(half), merged, replicas)
    mine = jnp.sum(exchange(keep + swap_cores(give), YX), axis=0) / replicas
    half = exchange(spread(mine, pairs), YX)

    ortho = ortho.T
    row_count = grads.shape[1] // replicas
    row_start = lax.axis_index(("y", "x", "core")) * row_count
    own = lax.dynamic_slice_in_dim(ortho, row_start, row_count, 0)
    update, right, new_errors = finish(core, half, swap_cores(half), ortho, own, merged)
    return update, right.T, new_errors[None]


def solution(mesh):
    chips = Mesh(mesh.devices.reshape(4, 4, 2, 8), ("y", "x", "core", "z"))
    dp = ("y", "x", "core")
    placed = (P(dp, None, "z"), P(dp, None, "z"), P("z", None))
    return jax.shard_map(
        per_device,
        mesh=chips,
        in_specs=placed,
        out_specs=(P(dp, "z"), P("z", None), P(dp, None, "z")),
        check_vma=False,
    )
```

```python
import jax
import jax.numpy as jnp
from jax import lax
from jax.experimental import pallas as pl
from jax.experimental.pallas import tpu as pltpu
from jax.sharding import Mesh, PartitionSpec as P

YX = ("y", "x")
VMEM_LIMIT = 32 * 1024 * 1024
WHOLE = pl.BlockSpec(memory_space=pltpu.VMEM)
SCALAR = pl.BlockSpec(memory_space=pltpu.SMEM)
ANYWHERE = pl.BlockSpec(memory_space=pl.ANY)
MERGE_CHUNK = 512
FINISH_CHUNK = 128
GROUP = 8


def own_first(core, low, high):
    return jnp.where(core == 0, low, high), jnp.where(core == 0, high, low)


def merge_kernel(core_ref, grads_ref, errors_ref, prior_ref, merged_ref, keep_ref, give_ref,
                 grads_held, errors_held, prior_held, sems, prior_sem):
    core = core_ref[0]
    rank = prior_ref.shape[0]
    rows = merged_ref.shape[0]
    chunks = rows // MERGE_CHUNK
    prior_fetch = pltpu.make_async_copy(prior_ref, prior_held, prior_sem)
    prior_fetch.start()
    fetches = []
    for i in range(chunks):
        block = pl.ds(MERGE_CHUNK * i, MERGE_CHUNK)
        pair = (
            pltpu.make_async_copy(grads_ref.at[block], grads_held.at[block], sems.at[0, i]),
            pltpu.make_async_copy(errors_ref.at[block], errors_held.at[block], sems.at[1, i]),
        )
        for fetch in pair:
            fetch.start()
        fetches.append(pair)
    for i in range(chunks):
        block = pl.ds(MERGE_CHUNK * i, MERGE_CHUNK)
        for fetch in fetches[i]:
            fetch.wait()
        merged = (
            grads_held[block].astype(jnp.float32) + errors_held[block].astype(jnp.float32)
        ).astype(jnp.bfloat16)
        merged_ref[block] = merged
        if i == 0:
            prior_fetch.wait()
            prior = prior_held[...].astype(jnp.bfloat16)
        left = lax.dot_general(
            prior, merged, (((1,), (1,)), ((), ())), preferred_element_type=jnp.float32
        )
        keep, give = own_first(core, left[: rank // 2], left[rank // 2 :])
        lanes = MERGE_CHUNK // 128
        for down in range(rank // 32):
            for lane in range(lanes):
                place = down * (rows // 128) + i * lanes + lane
                tile = (slice(16 * down, 16 * down + 16), slice(128 * lane, 128 * lane + 128))
                keep_ref[place] = keep[tile]
                give_ref[place] = give[tile]


def merge(core, grads, errors, prior):
    rows, columns = grads.shape
    rank = prior.shape[0]
    tiles = jax.ShapeDtypeStruct((rows // 128 * (rank // 32), 16, 128), jnp.float32)
    return pl.pallas_call(
        merge_kernel,
        in_specs=[SCALAR, ANYWHERE, ANYWHERE, ANYWHERE],
        out_specs=[WHOLE, WHOLE, WHOLE],
        out_shape=[pltpu.VMEM(grads.shape, jnp.bfloat16), tiles, tiles],
        scratch_shapes=[
            pltpu.VMEM(grads.shape, jnp.bfloat16),
            pltpu.VMEM(grads.shape, jnp.bfloat16),
            pltpu.VMEM(prior.shape, jnp.float32),
            pltpu.SemaphoreType.DMA((2, rows // MERGE_CHUNK)),
            pltpu.SemaphoreType.DMA,
        ],
        compiler_params=pltpu.CompilerParams(vmem_limit_bytes=VMEM_LIMIT),
        cost_estimate=pl.CostEstimate(
            flops=2 * rows * columns * rank, bytes_accessed=6 * rows * columns, transcendentals=0
        ),
    )(core, *[pltpu.with_memory_space_constraint(x, pltpu.HBM) for x in (grads, errors, prior)])


def inverse_factor(gram):
    rank = gram.shape[0]
    shape = (GROUP, 2 * rank)
    row = lax.broadcasted_iota(jnp.int32, (rank, rank), 0)
    column = lax.broadcasted_iota(jnp.int32, (rank, rank), 1)
    state = jnp.concatenate([gram, jnp.where(row == column, 1.0, 0.0)], axis=1)
    groups = [state[GROUP * g : GROUP * g + GROUP] for g in range(rank // GROUP)]
    place = lax.broadcasted_iota(jnp.int32, shape, 0)
    span = range(GROUP)
    for own in range(rank // GROUP):
        later = range(own, rank // GROUP)
        first = GROUP * own
        columns = [
            {g: jnp.broadcast_to(groups[g][:, first + j : first + j + 1], shape) for g in later}
            for j in span
        ]
        rows = [jnp.broadcast_to(groups[own][j : j + 1], shape) for j in span]
        cross = [
            [jnp.broadcast_to(columns[j][own][i : i + 1], shape) for j in range(i + 1)] for i in span
        ]
        for j in span:
            scale = lax.rsqrt(cross[j][j])
            rows[j] = rows[j] * scale
            for g in later:
                columns[j][g] = columns[j][g] * scale
            for i in range(j + 1, GROUP):
                cross[i][j] = cross[i][j] * scale
            for i in range(j + 1, GROUP):
                rows[i] = rows[i] - cross[i][j] * rows[j]
                for g in later:
                    columns[i][g] = columns[i][g] - columns[j][g] * cross[i][j]
                for l in range(j + 1, i + 1):
                    cross[i][l] = cross[i][l] - cross[i][j] * cross[l][j]
        for g in range(own + 1, rank // GROUP):
            for j in span:
                groups[g] = groups[g] - columns[j][g] * rows[j]
        groups[own] = rows[0]
        for j in range(1, GROUP):
            groups[own] = jnp.where(place == j, rows[j], groups[own])
    return jnp.concatenate(groups)[:, rank:]


def ortho_kernel(core_ref, half_ref, other_ref, merged_ref, ortho_ref, keep_ref, give_ref,
                 left_ref):
    core = core_ref[0]
    rank, rows = left_ref.shape
    across = rows // 128
    for place in range(half_ref.shape[0]):
        low, high = own_first(core, half_ref[place], other_ref[place])
        down = 16 * (place // across)
        lane = pl.ds(128 * (place % across), 128)
        left_ref[pl.ds(down, 16), lane] = low
        left_ref[pl.ds(rank // 2 + down, 16), lane] = high
    left = left_ref[...]
    gram = lax.dot_general(
        left, left, (((1,), (1,)), ((), ())), precision=lax.Precision.HIGHEST,
        preferred_element_type=jnp.float32,
    )
    ortho = jnp.dot(
        inverse_factor(gram), left, precision=lax.Precision.HIGHEST,
        preferred_element_type=jnp.float32,
    ).astype(jnp.bfloat16)
    ortho_ref[...] = ortho
    wide = keep_ref.shape[2]
    count = merged_ref.shape[1] // wide
    for lane in range(count):
        right = jnp.dot(
            ortho, merged_ref[:, wide * lane : wide * lane + wide],
            preferred_element_type=jnp.float32,
        )
        keep, give = own_first(core, right[: rank // 2], right[rank // 2 :])
        for down in range(rank // 16):
            keep_ref[down * count + lane] = keep[8 * down : 8 * down + 8]
            give_ref[down * count + lane] = give[8 * down : 8 * down + 8]


def orthonormal(core, half, other, merged, parts):
    rows, columns = merged.shape
    rank = half.size * 2 // rows
    wide = rank * columns // (8 * parts)
    tiles = jax.ShapeDtypeStruct((parts // 2, 8, wide), jnp.float32)
    return pl.pallas_call(
        ortho_kernel,
        in_specs=[SCALAR, WHOLE, WHOLE, WHOLE],
        out_specs=[WHOLE, WHOLE, WHOLE],
        out_shape=[jax.ShapeDtypeStruct((rank, rows), jnp.bfloat16), tiles, tiles],
        scratch_shapes=[pltpu.VMEM((rank, rows), jnp.float32)],
        compiler_params=pltpu.CompilerParams(vmem_limit_bytes=VMEM_LIMIT),
        cost_estimate=pl.CostEstimate(
            flops=2 * rows * columns * rank, bytes_accessed=2 * rows * columns, transcendentals=0
        ),
    )(core, half, other, merged)


def finish_kernel(core_ref, half_ref, other_ref, ortho_ref, own_ref, merged_ref,
                  update_ref, right_ref, errors_ref, cast_ref, errors_held, sems):
    core = core_ref[0]
    rank = ortho_ref.shape[1]
    wide = half_ref.shape[2]
    count = right_ref.shape[1] // wide
    for lane in range(count):
        pairs = [
            own_first(core, half_ref[down * count + lane], other_ref[down * count + lane])
            for down in range(rank // 16)
        ]
        right = jnp.concatenate([low for low, _ in pairs] + [high for _, high in pairs])
        cast_ref[:, wide * lane : wide * lane + wide] = right.astype(jnp.bfloat16)
        right_ref[:, wide * lane : wide * lane + wide] = right
    cast = cast_ref[...]
    stores = []
    for i in range(merged_ref.shape[0] // FINISH_CHUNK):
        block = pl.ds(FINISH_CHUNK * i, FINISH_CHUNK)
        full_update = jnp.dot(ortho_ref[block], cast, preferred_element_type=jnp.float32)
        errors_held[block] = (
            merged_ref[block].astype(jnp.float32) - full_update
        ).astype(jnp.bfloat16)
        store = pltpu.make_async_copy(errors_held.at[block], errors_ref.at[block], sems.at[i])
        store.start()
        stores.append(store)
    update_ref[...] = jnp.dot(
        own_ref[...], cast, preferred_element_type=jnp.float32
    ).astype(jnp.bfloat16)
    for store in stores:
        store.wait()


def finish(core, half, other, ortho, own, merged):
    rows, columns = merged.shape
    rank = ortho.shape[1]
    return pl.pallas_call(
        finish_kernel,
        in_specs=[SCALAR, WHOLE, WHOLE, WHOLE, WHOLE, WHOLE],
        out_specs=[WHOLE, WHOLE, ANYWHERE],
        out_shape=[
            jax.ShapeDtypeStruct((own.shape[0], columns), jnp.bfloat16),
            jax.ShapeDtypeStruct((rank, columns), jnp.float32),
            jax.ShapeDtypeStruct(merged.shape, jnp.bfloat16),
        ],
        scratch_shapes=[
            pltpu.VMEM((rank, columns), jnp.bfloat16),
            pltpu.VMEM(merged.shape, jnp.bfloat16),
            pltpu.SemaphoreType.DMA((rows // FINISH_CHUNK,)),
        ],
        compiler_params=pltpu.CompilerParams(vmem_limit_bytes=VMEM_LIMIT),
        cost_estimate=pl.CostEstimate(
            flops=2 * rows * columns * rank, bytes_accessed=4 * rows * columns, transcendentals=0
        ),
    )(core, half, other, ortho, own, merged)


def swap_cores(value):
    return lax.ppermute(value, "core", [(0, 1), (1, 0)])


def exchange(value, axes):
    return lax.all_to_all(value, axes, 0, 0)


def spread(value, copies):
    return jnp.broadcast_to(value[None], (copies,) + value.shape)


def per_device(grads, errors, q_prev):
    core = lax.axis_index("core").astype(jnp.int32).reshape(1)
    pairs = lax.axis_size("y") * lax.axis_size("x")
    depth = lax.axis_size("z")
    replicas = 2 * pairs

    merged, keep, give = merge(core, grads[0], errors[0], q_prev.T)
    mine = jnp.sum(exchange(keep + swap_cores(give), YX), axis=0)
    mine = jnp.sum(exchange(spread(mine, depth), "z"), axis=0) / replicas
    half = exchange(spread(mine, pairs), YX)

    ortho, keep, give = orthonormal(core, half, swap_cores(half), merged, replicas)
    mine = jnp.sum(exchange(keep + swap_cores(give), YX), axis=0) / replicas
    half = exchange(spread(mine, pairs), YX)

    ortho = ortho.T
    row_count = grads.shape[1] // replicas
    row_start = lax.axis_index(("y", "x", "core")) * row_count
    own = lax.dynamic_slice_in_dim(ortho, row_start, row_count, 0)
    update, right, new_errors = finish(core, half, swap_cores(half), ortho, own, merged)
    return update, right.T, new_errors[None]


def solution(mesh):
    chips = Mesh(mesh.devices.reshape(4, 4, 2, 8), ("y", "x", "core", "z"))
    dp = ("y", "x", "core")
    placed = (P(dp, None, "z"), P(dp, None, "z"), P("z", None))
    return jax.shard_map(
        per_device,
        mesh=chips,
        in_specs=placed,
        out_specs=(P(dp, "z"), P("z", None), P(dp, None, "z")),
        check_vma=False,
    )
```

```python
import jax
import jax.numpy as jnp
from jax import lax
from jax.experimental import pallas as pl
from jax.experimental.pallas import tpu as pltpu
from jax.sharding import Mesh, PartitionSpec as P

YX = ("y", "x")
VMEM_LIMIT = 32 * 1024 * 1024
WHOLE = pl.BlockSpec(memory_space=pltpu.VMEM)
SCALAR = pl.BlockSpec(memory_space=pltpu.SMEM)
ANYWHERE = pl.BlockSpec(memory_space=pl.ANY)
MERGE_CHUNK = 512
FINISH_CHUNK = 128
GROUP = 8


def own_first(core, low, high):
    return jnp.where(core == 0, low, high), jnp.where(core == 0, high, low)


def merge_kernel(grads_ref, errors_ref, prior_ref, merged_ref, left_ref,
                 grads_held, errors_held, prior_held, sems, prior_sem):
    rank = prior_ref.shape[0]
    rows = merged_ref.shape[0]
    chunks = rows // MERGE_CHUNK
    prior_fetch = pltpu.make_async_copy(prior_ref, prior_held, prior_sem)
    prior_fetch.start()
    fetches = []
    for i in range(chunks):
        block = pl.ds(MERGE_CHUNK * i, MERGE_CHUNK)
        pair = (
            pltpu.make_async_copy(grads_ref.at[block], grads_held.at[block], sems.at[0, i]),
            pltpu.make_async_copy(errors_ref.at[block], errors_held.at[block], sems.at[1, i]),
        )
        for fetch in pair:
            fetch.start()
        fetches.append(pair)
    for i in range(chunks):
        block = pl.ds(MERGE_CHUNK * i, MERGE_CHUNK)
        for fetch in fetches[i]:
            fetch.wait()
        merged = (
            grads_held[block].astype(jnp.float32) + errors_held[block].astype(jnp.float32)
        ).astype(jnp.bfloat16)
        merged_ref[block] = merged
        if i == 0:
            prior_fetch.wait()
            prior = prior_held[...].astype(jnp.bfloat16)
        left = lax.dot_general(
            prior, merged, (((1,), (1,)), ((), ())), preferred_element_type=jnp.float32
        )
        lanes = MERGE_CHUNK // 128
        for down in range(rank // 16):
            half, place = divmod(down, rank // 32)
            for lane in range(lanes):
                left_ref[place * (rows // 128) + i * lanes + lane, 16 * half : 16 * half + 16] = (
                    left[16 * down : 16 * down + 16, 128 * lane : 128 * lane + 128]
                )


def merge(grads, errors, prior):
    rows, columns = grads.shape
    rank = prior.shape[0]
    tiles = jax.ShapeDtypeStruct((rows // 128 * (rank // 32), 32, 128), jnp.float32)
    return pl.pallas_call(
        merge_kernel,
        in_specs=[ANYWHERE, ANYWHERE, ANYWHERE],
        out_specs=[WHOLE, WHOLE],
        out_shape=[pltpu.VMEM(grads.shape, jnp.bfloat16), tiles],
        scratch_shapes=[
            pltpu.VMEM(grads.shape, jnp.bfloat16),
            pltpu.VMEM(grads.shape, jnp.bfloat16),
            pltpu.VMEM(prior.shape, jnp.float32),
            pltpu.SemaphoreType.DMA((2, rows // MERGE_CHUNK)),
            pltpu.SemaphoreType.DMA,
        ],
        compiler_params=pltpu.CompilerParams(vmem_limit_bytes=VMEM_LIMIT),
        cost_estimate=pl.CostEstimate(
            flops=2 * rows * columns * rank, bytes_accessed=6 * rows * columns, transcendentals=0
        ),
    )(*[pltpu.with_memory_space_constraint(x, pltpu.HBM) for x in (grads, errors, prior)])


def inverse_factor(gram):
    rank = gram.shape[0]
    shape = (GROUP, 2 * rank)
    row = lax.broadcasted_iota(jnp.int32, (rank, rank), 0)
    column = lax.broadcasted_iota(jnp.int32, (rank, rank), 1)
    state = jnp.concatenate([gram, jnp.where(row == column, 1.0, 0.0)], axis=1)
    groups = [state[GROUP * g : GROUP * g + GROUP] for g in range(rank // GROUP)]
    place = lax.broadcasted_iota(jnp.int32, shape, 0)
    span = range(GROUP)
    for own in range(rank // GROUP):
        later = range(own, rank // GROUP)
        first = GROUP * own
        columns = [
            {g: jnp.broadcast_to(groups[g][:, first + j : first + j + 1], shape) for g in later}
            for j in span
        ]
        rows = [jnp.broadcast_to(groups[own][j : j + 1], shape) for j in span]
        cross = [
            [jnp.broadcast_to(columns[j][own][i : i + 1], shape) for j in range(i + 1)] for i in span
        ]
        for j in span:
            scale = lax.rsqrt(cross[j][j])
            rows[j] = rows[j] * scale
            for g in later:
                columns[j][g] = columns[j][g] * scale
            for i in range(j + 1, GROUP):
                cross[i][j] = cross[i][j] * scale
            for i in range(j + 1, GROUP):
                rows[i] = rows[i] - cross[i][j] * rows[j]
                for g in later:
                    columns[i][g] = columns[i][g] - columns[j][g] * cross[i][j]
                for l in range(j + 1, i + 1):
                    cross[i][l] = cross[i][l] - cross[i][j] * cross[l][j]
        for g in range(own + 1, rank // GROUP):
            for j in span:
                groups[g] = groups[g] - columns[j][g] * rows[j]
        groups[own] = rows[0]
        for j in range(1, GROUP):
            groups[own] = jnp.where(place == j, rows[j], groups[own])
    return jnp.concatenate(groups)[:, rank:]


def ortho_kernel(core_ref, own_ref, other_ref, merged_ref, ortho_ref, keep_ref, give_ref,
                 left_ref):
    core = core_ref[0]
    rank, rows = left_ref.shape
    across = rows // 128
    for place in range(own_ref.shape[0]):
        tile = jnp.where(core == 1, own_ref[place], other_ref[place])
        lane = pl.ds(128 * (place % across), 128)
        for half in range(2):
            down = rank // 2 * half + 16 * (place // across)
            left_ref[pl.ds(down, 16), lane] = tile[16 * half : 16 * half + 16]
    left = left_ref[...]
    gram = lax.dot_general(
        left, left, (((1,), (1,)), ((), ())), precision=lax.Precision.HIGHEST,
        preferred_element_type=jnp.float32,
    )
    ortho = jnp.dot(
        inverse_factor(gram), left, precision=lax.Precision.HIGHEST,
        preferred_element_type=jnp.float32,
    ).astype(jnp.bfloat16)
    ortho_ref[...] = ortho
    wide = keep_ref.shape[2]
    count = merged_ref.shape[1] // wide
    for lane in range(count):
        right = jnp.dot(
            ortho, merged_ref[:, wide * lane : wide * lane + wide],
            preferred_element_type=jnp.float32,
        )
        keep, give = own_first(core, right[: rank // 2], right[rank // 2 :])
        for down in range(rank // 16):
            keep_ref[down * count + lane] = keep[8 * down : 8 * down + 8]
            give_ref[down * count + lane] = give[8 * down : 8 * down + 8]


def orthonormal(core, own, other, merged, parts):
    rows, columns = merged.shape
    rank = own.size // rows
    wide = rank * columns // (8 * parts)
    tiles = jax.ShapeDtypeStruct((parts // 2, 8, wide), jnp.float32)
    return pl.pallas_call(
        ortho_kernel,
        in_specs=[SCALAR, WHOLE, WHOLE, WHOLE],
        out_specs=[WHOLE, WHOLE, WHOLE],
        out_shape=[jax.ShapeDtypeStruct((rank, rows), jnp.bfloat16), tiles, tiles],
        scratch_shapes=[pltpu.VMEM((rank, rows), jnp.float32)],
        compiler_params=pltpu.CompilerParams(vmem_limit_bytes=VMEM_LIMIT),
        cost_estimate=pl.CostEstimate(
            flops=2 * rows * columns * rank, bytes_accessed=2 * rows * columns, transcendentals=0
        ),
    )(core, own, other, merged)


def finish_kernel(core_ref, half_ref, other_ref, ortho_ref, own_ref, merged_ref,
                  update_ref, right_ref, errors_ref, cast_ref, errors_held, sems):
    core = core_ref[0]
    rank = ortho_ref.shape[1]
    wide = half_ref.shape[2]
    count = right_ref.shape[1] // wide
    for lane in range(count):
        pairs = [
            own_first(core, half_ref[down * count + lane], other_ref[down * count + lane])
            for down in range(rank // 16)
        ]
        right = jnp.concatenate([low for low, _ in pairs] + [high for _, high in pairs])
        cast_ref[:, wide * lane : wide * lane + wide] = right.astype(jnp.bfloat16)
        right_ref[:, wide * lane : wide * lane + wide] = right
    cast = cast_ref[...]
    stores = []
    for i in range(merged_ref.shape[0] // FINISH_CHUNK):
        block = pl.ds(FINISH_CHUNK * i, FINISH_CHUNK)
        full_update = jnp.dot(ortho_ref[block], cast, preferred_element_type=jnp.float32)
        errors_held[block] = (
            merged_ref[block].astype(jnp.float32) - full_update
        ).astype(jnp.bfloat16)
        store = pltpu.make_async_copy(errors_held.at[block], errors_ref.at[block], sems.at[i])
        store.start()
        stores.append(store)
    update_ref[...] = jnp.dot(
        own_ref[...], cast, preferred_element_type=jnp.float32
    ).astype(jnp.bfloat16)
    for store in stores:
        store.wait()


def finish(core, half, other, ortho, own, merged):
    rows, columns = merged.shape
    rank = ortho.shape[1]
    return pl.pallas_call(
        finish_kernel,
        in_specs=[SCALAR, WHOLE, WHOLE, WHOLE, WHOLE, WHOLE],
        out_specs=[WHOLE, WHOLE, ANYWHERE],
        out_shape=[
            jax.ShapeDtypeStruct((own.shape[0], columns), jnp.bfloat16),
            jax.ShapeDtypeStruct((rank, columns), jnp.float32),
            jax.ShapeDtypeStruct(merged.shape, jnp.bfloat16),
        ],
        scratch_shapes=[
            pltpu.VMEM((rank, columns), jnp.bfloat16),
            pltpu.VMEM(merged.shape, jnp.bfloat16),
            pltpu.SemaphoreType.DMA((rows // FINISH_CHUNK,)),
        ],
        compiler_params=pltpu.CompilerParams(vmem_limit_bytes=VMEM_LIMIT),
        cost_estimate=pl.CostEstimate(
            flops=2 * rows * columns * rank, bytes_accessed=4 * rows * columns, transcendentals=0
        ),
    )(core, half, other, ortho, own, merged)


def swap_cores(value):
    return lax.ppermute(value, "core", [(0, 1), (1, 0)])


def exchange(value, axes):
    return lax.all_to_all(value, axes, 0, 0)


def spread(value, copies):
    return jnp.broadcast_to(value[None], (copies,) + value.shape)


def per_device(grads, errors, q_prev):
    core = lax.axis_index("core").astype(jnp.int32).reshape(1)
    pairs = lax.axis_size("y") * lax.axis_size("x")
    depth = lax.axis_size("z")
    replicas = 2 * pairs

    def reduce_left(total):
        mine = jnp.sum(exchange(total, YX), axis=0)
        mine = jnp.sum(exchange(spread(mine, depth), "z"), axis=0) / replicas
        return exchange(spread(mine, pairs), YX)

    merged, left = merge(grads[0], errors[0], q_prev.T)
    left = lax.cond(core[0] == 1, reduce_left, lambda total: total, left + swap_cores(left))

    ortho, keep, give = orthonormal(core, left, swap_cores(left), merged, replicas)
    mine = jnp.sum(exchange(keep + swap_cores(give), YX), axis=0) / replicas
    half = exchange(spread(mine, pairs), YX)

    ortho = ortho.T
    row_count = grads.shape[1] // replicas
    row_start = lax.axis_index(("y", "x", "core")) * row_count
    own = lax.dynamic_slice_in_dim(ortho, row_start, row_count, 0)
    update, right, new_errors = finish(core, half, swap_cores(half), ortho, own, merged)
    return update, right.T, new_errors[None]


def solution(mesh):
    chips = Mesh(mesh.devices.reshape(4, 4, 2, 8), ("y", "x", "core", "z"))
    dp = ("y", "x", "core")
    placed = (P(dp, None, "z"), P(dp, None, "z"), P("z", None))
    return jax.shard_map(
        per_device,
        mesh=chips,
        in_specs=placed,
        out_specs=(P(dp, "z"), P("z", None), P(dp, None, "z")),
        check_vma=False,
    )
```

```python
import jax
import jax.numpy as jnp
from jax import lax
from jax.experimental import pallas as pl
from jax.experimental.pallas import tpu as pltpu
from jax.sharding import Mesh, PartitionSpec as P

YX = ("y", "x")
VMEM_LIMIT = 32 * 1024 * 1024
WHOLE = pl.BlockSpec(memory_space=pltpu.VMEM)
SCALAR = pl.BlockSpec(memory_space=pltpu.SMEM)
ANYWHERE = pl.BlockSpec(memory_space=pl.ANY)
MERGE_CHUNK = 512
FINISH_CHUNK = 128
GROUP = 8


def in_vmem(value):
    return pltpu.with_memory_space_constraint(value, pltpu.VMEM)


def own_first(core, low, high):
    return jnp.where(core == 0, low, high), jnp.where(core == 0, high, low)


def merge_kernel(core_ref, grads_ref, errors_ref, prior_ref, merged_ref, keep_ref, give_ref,
                 grads_held, errors_held, prior_held, sems, prior_sem):
    core = core_ref[0]
    rank = prior_ref.shape[0]
    rows = merged_ref.shape[0]
    chunks = rows // MERGE_CHUNK
    prior_fetch = pltpu.make_async_copy(prior_ref, prior_held, prior_sem)
    prior_fetch.start()
    fetches = []
    for i in range(chunks):
        block = pl.ds(MERGE_CHUNK * i, MERGE_CHUNK)
        pair = (
            pltpu.make_async_copy(grads_ref.at[block], grads_held.at[block], sems.at[0, i]),
            pltpu.make_async_copy(errors_ref.at[block], errors_held.at[block], sems.at[1, i]),
        )
        for fetch in pair:
            fetch.start()
        fetches.append(pair)
    for i in range(chunks):
        block = pl.ds(MERGE_CHUNK * i, MERGE_CHUNK)
        for fetch in fetches[i]:
            fetch.wait()
        merged = (
            grads_held[block].astype(jnp.float32) + errors_held[block].astype(jnp.float32)
        ).astype(jnp.bfloat16)
        merged_ref[block] = merged
        if i == 0:
            prior_fetch.wait()
            prior = prior_held[...].astype(jnp.bfloat16)
        left = lax.dot_general(
            prior, merged, (((1,), (1,)), ((), ())), preferred_element_type=jnp.float32
        )
        keep, give = own_first(core, left[: rank // 2], left[rank // 2 :])
        lanes = MERGE_CHUNK // 128
        for down in range(rank // 32):
            for lane in range(lanes):
                place = down * (rows // 128) + i * lanes + lane
                tile = (slice(16 * down, 16 * down + 16), slice(128 * lane, 128 * lane + 128))
                keep_ref[place] = keep[tile]
                give_ref[place] = give[tile]


def merge(core, grads, errors, prior):
    rows, columns = grads.shape
    rank = prior.shape[0]
    tiles = jax.ShapeDtypeStruct((rows // 128 * (rank // 32), 16, 128), jnp.float32)
    return pl.pallas_call(
        merge_kernel,
        in_specs=[SCALAR, ANYWHERE, ANYWHERE, ANYWHERE],
        out_specs=[WHOLE, WHOLE, WHOLE],
        out_shape=[pltpu.VMEM(grads.shape, jnp.bfloat16), tiles, tiles],
        scratch_shapes=[
            pltpu.VMEM(grads.shape, jnp.bfloat16),
            pltpu.VMEM(grads.shape, jnp.bfloat16),
            pltpu.VMEM(prior.shape, jnp.float32),
            pltpu.SemaphoreType.DMA((2, rows // MERGE_CHUNK)),
            pltpu.SemaphoreType.DMA,
        ],
        compiler_params=pltpu.CompilerParams(vmem_limit_bytes=VMEM_LIMIT),
        cost_estimate=pl.CostEstimate(
            flops=2 * rows * columns * rank, bytes_accessed=6 * rows * columns, transcendentals=0
        ),
    )(core, *[pltpu.with_memory_space_constraint(x, pltpu.HBM) for x in (grads, errors, prior)])


def inverse_factor(gram):
    rank = gram.shape[0]
    shape = (GROUP, 2 * rank)
    row = lax.broadcasted_iota(jnp.int32, (rank, rank), 0)
    column = lax.broadcasted_iota(jnp.int32, (rank, rank), 1)
    state = jnp.concatenate([gram, jnp.where(row == column, 1.0, 0.0)], axis=1)
    groups = [state[GROUP * g : GROUP * g + GROUP] for g in range(rank // GROUP)]
    place = lax.broadcasted_iota(jnp.int32, shape, 0)
    span = range(GROUP)
    for own in range(rank // GROUP):
        later = range(own, rank // GROUP)
        first = GROUP * own
        columns = [
            {g: jnp.broadcast_to(groups[g][:, first + j : first + j + 1], shape) for g in later}
            for j in span
        ]
        rows = [jnp.broadcast_to(groups[own][j : j + 1], shape) for j in span]
        cross = [
            [jnp.broadcast_to(columns[j][own][i : i + 1], shape) for j in range(i + 1)] for i in span
        ]
        for j in span:
            scale = lax.rsqrt(cross[j][j])
            rows[j] = rows[j] * scale
            for g in later:
                columns[j][g] = columns[j][g] * scale
            for i in range(j + 1, GROUP):
                cross[i][j] = cross[i][j] * scale
            for i in range(j + 1, GROUP):
                rows[i] = rows[i] - cross[i][j] * rows[j]
                for g in later:
                    columns[i][g] = columns[i][g] - columns[j][g] * cross[i][j]
                for l in range(j + 1, i + 1):
                    cross[i][l] = cross[i][l] - cross[i][j] * cross[l][j]
        for g in range(own + 1, rank // GROUP):
            for j in span:
                groups[g] = groups[g] - columns[j][g] * rows[j]
        groups[own] = rows[0]
        for j in range(1, GROUP):
            groups[own] = jnp.where(place == j, rows[j], groups[own])
    return jnp.concatenate(groups)[:, rank:]


def ortho_kernel(core_ref, half_ref, other_ref, merged_ref, ortho_ref, keep_ref, give_ref,
                 left_ref):
    core = core_ref[0]
    rank, rows = left_ref.shape
    across = rows // 128
    for place in range(half_ref.shape[0]):
        low, high = own_first(core, half_ref[place], other_ref[place])
        down = 16 * (place // across)
        lane = pl.ds(128 * (place % across), 128)
        left_ref[pl.ds(down, 16), lane] = low
        left_ref[pl.ds(rank // 2 + down, 16), lane] = high
    left = left_ref[...]
    gram = lax.dot_general(
        left, left, (((1,), (1,)), ((), ())), precision=lax.Precision.HIGHEST,
        preferred_element_type=jnp.float32,
    )
    ortho = jnp.dot(
        inverse_factor(gram), left, precision=lax.Precision.HIGHEST,
        preferred_element_type=jnp.float32,
    ).astype(jnp.bfloat16)
    ortho_ref[...] = ortho
    wide = keep_ref.shape[2]
    count = merged_ref.shape[1] // wide
    for lane in range(count):
        right = jnp.dot(
            ortho, merged_ref[:, wide * lane : wide * lane + wide],
            preferred_element_type=jnp.float32,
        )
        keep, give = own_first(core, right[: rank // 2], right[rank // 2 :])
        for down in range(rank // 16):
            keep_ref[down * count + lane] = keep[8 * down : 8 * down + 8]
            give_ref[down * count + lane] = give[8 * down : 8 * down + 8]


def orthonormal(core, half, other, merged, parts):
    rows, columns = merged.shape
    rank = half.size * 2 // rows
    wide = rank * columns // (8 * parts)
    tiles = jax.ShapeDtypeStruct((parts // 2, 8, wide), jnp.float32)
    return pl.pallas_call(
        ortho_kernel,
        in_specs=[SCALAR, WHOLE, WHOLE, WHOLE],
        out_specs=[WHOLE, WHOLE, WHOLE],
        out_shape=[jax.ShapeDtypeStruct((rank, rows), jnp.bfloat16), tiles, tiles],
        scratch_shapes=[pltpu.VMEM((rank, rows), jnp.float32)],
        compiler_params=pltpu.CompilerParams(vmem_limit_bytes=VMEM_LIMIT),
        cost_estimate=pl.CostEstimate(
            flops=2 * rows * columns * rank, bytes_accessed=2 * rows * columns, transcendentals=0
        ),
    )(core, half, other, merged)


def finish_kernel(core_ref, half_ref, other_ref, ortho_ref, own_ref, merged_ref,
                  update_ref, right_ref, errors_ref,
                  cast_ref, update_held, right_held, errors_held, small_sems, sems):
    core = core_ref[0]
    rank = ortho_ref.shape[1]
    wide = half_ref.shape[2]
    count = right_ref.shape[1] // wide
    for lane in range(count):
        pairs = [
            own_first(core, half_ref[down * count + lane], other_ref[down * count + lane])
            for down in range(rank // 16)
        ]
        right = jnp.concatenate([low for low, _ in pairs] + [high for _, high in pairs])
        cast_ref[:, wide * lane : wide * lane + wide] = right.astype(jnp.bfloat16)
        right_held[:, wide * lane : wide * lane + wide] = right
    cast = cast_ref[...]
    stores = []
    for i in range(merged_ref.shape[0] // FINISH_CHUNK):
        block = pl.ds(FINISH_CHUNK * i, FINISH_CHUNK)
        full_update = jnp.dot(ortho_ref[block], cast, preferred_element_type=jnp.float32)
        errors_held[block] = (
            merged_ref[block].astype(jnp.float32) - full_update
        ).astype(jnp.bfloat16)
        stores.append(
            pltpu.make_async_copy(errors_held.at[block], errors_ref.at[block], sems.at[i])
        )
        stores[-1].start()
        if i == 0:
            stores.append(pltpu.make_async_copy(right_held, right_ref, small_sems.at[0]))
            stores[-1].start()
            update_held[...] = jnp.dot(
                own_ref[...], cast, preferred_element_type=jnp.float32
            ).astype(jnp.bfloat16)
            stores.append(pltpu.make_async_copy(update_held, update_ref, small_sems.at[1]))
            stores[-1].start()
    for store in stores:
        store.wait()


def finish(core, half, other, ortho, own, merged):
    rows, columns = merged.shape
    rank = ortho.shape[1]
    small = (own.shape[0], columns), (rank, columns)
    return pl.pallas_call(
        finish_kernel,
        in_specs=[SCALAR, WHOLE, WHOLE, WHOLE, WHOLE, WHOLE],
        out_specs=[ANYWHERE, ANYWHERE, ANYWHERE],
        out_shape=[
            pltpu.HBM(small[0], jnp.bfloat16),
            pltpu.HBM(small[1], jnp.float32),
            pltpu.HBM(merged.shape, jnp.bfloat16),
        ],
        scratch_shapes=[
            pltpu.VMEM(small[1], jnp.bfloat16),
            pltpu.VMEM(small[0], jnp.bfloat16),
            pltpu.VMEM(small[1], jnp.float32),
            pltpu.VMEM(merged.shape, jnp.bfloat16),
            pltpu.SemaphoreType.DMA((2,)),
            pltpu.SemaphoreType.DMA((rows // FINISH_CHUNK,)),
        ],
        compiler_params=pltpu.CompilerParams(vmem_limit_bytes=VMEM_LIMIT),
        cost_estimate=pl.CostEstimate(
            flops=2 * rows * columns * rank, bytes_accessed=4 * rows * columns, transcendentals=0
        ),
    )(core, in_vmem(half), in_vmem(other), ortho, own, merged)


def swap_cores(value):
    return lax.ppermute(value, "core", [(0, 1), (1, 0)])


def exchange(value, axes):
    return lax.all_to_all(value, axes, 0, 0)


def spread(value, copies):
    return jnp.broadcast_to(value[None], (copies,) + value.shape)


def per_device(grads, errors, q_prev):
    core = lax.axis_index("core").astype(jnp.int32).reshape(1)
    pairs = lax.axis_size("y") * lax.axis_size("x")
    depth = lax.axis_size("z")
    replicas = 2 * pairs

    merged, keep, give = merge(core, grads[0], errors[0], q_prev.T)
    mine = jnp.sum(exchange(keep + swap_cores(give), YX), axis=0)
    mine = jnp.sum(exchange(spread(mine, depth), "z"), axis=0) / replicas
    half = exchange(spread(mine, pairs), YX)

    ortho, keep, give = orthonormal(core, half, swap_cores(half), merged, replicas)
    mine = jnp.sum(exchange(keep + swap_cores(give), YX), axis=0) / replicas
    half = exchange(spread(mine, pairs), YX)

    ortho = ortho.T
    row_count = grads.shape[1] // replicas
    row_start = lax.axis_index(("y", "x", "core")) * row_count
    own = lax.dynamic_slice_in_dim(ortho, row_start, row_count, 0)
    update, right, new_errors = finish(core, half, swap_cores(half), ortho, own, merged)
    return update, right.T, new_errors[None]


def solution(mesh):
    chips = Mesh(mesh.devices.reshape(4, 4, 2, 8), ("y", "x", "core", "z"))
    dp = ("y", "x", "core")
    placed = (P(dp, None, "z"), P(dp, None, "z"), P("z", None))
    return jax.shard_map(
        per_device,
        mesh=chips,
        in_specs=placed,
        out_specs=(P(dp, "z"), P("z", None), P(dp, None, "z")),
        check_vma=False,
    )
```

```python
import jax
import jax.numpy as jnp
from jax import lax
from jax.experimental import pallas as pl
from jax.experimental.pallas import tpu as pltpu
from jax.sharding import Mesh, PartitionSpec as P

YX = ("y", "x")
VMEM_LIMIT = 32 * 1024 * 1024
WHOLE = pl.BlockSpec(memory_space=pltpu.VMEM)
SCALAR = pl.BlockSpec(memory_space=pltpu.SMEM)
ANYWHERE = pl.BlockSpec(memory_space=pl.ANY)
MERGE_CHUNK = 512
FINISH_CHUNK = 128
GROUP = 8


def own_first(core, low, high):
    return jnp.where(core == 0, low, high), jnp.where(core == 0, high, low)


def merge_kernel(core_ref, grads_ref, errors_ref, prior_ref, merged_ref, keep_ref, give_ref,
                 grads_held, errors_held, prior_held, sems, prior_sem):
    core = core_ref[0]
    rank = prior_ref.shape[0]
    rows = merged_ref.shape[0]
    chunks = rows // MERGE_CHUNK
    prior_fetch = pltpu.make_async_copy(prior_ref, prior_held, prior_sem)
    prior_fetch.start()
    fetches = []
    for i in range(chunks):
        block = pl.ds(MERGE_CHUNK * i, MERGE_CHUNK)
        pair = (
            pltpu.make_async_copy(grads_ref.at[block], grads_held.at[block], sems.at[0, i]),
            pltpu.make_async_copy(errors_ref.at[block], errors_held.at[block], sems.at[1, i]),
        )
        for fetch in pair:
            fetch.start()
        fetches.append(pair)
    for i in range(chunks):
        block = pl.ds(MERGE_CHUNK * i, MERGE_CHUNK)
        for fetch in fetches[i]:
            fetch.wait()
        merged = (
            grads_held[block].astype(jnp.float32) + errors_held[block].astype(jnp.float32)
        ).astype(jnp.bfloat16)
        merged_ref[block] = merged
        if i == 0:
            prior_fetch.wait()
            prior = prior_held[...].astype(jnp.bfloat16)
        left = lax.dot_general(
            prior, merged, (((1,), (1,)), ((), ())), preferred_element_type=jnp.float32
        )
        keep, give = own_first(core, left[: rank // 2], left[rank // 2 :])
        lanes = MERGE_CHUNK // 128
        for down in range(rank // 32):
            for lane in range(lanes):
                place = down * (rows // 128) + i * lanes + lane
                tile = (slice(16 * down, 16 * down + 16), slice(128 * lane, 128 * lane + 128))
                keep_ref[place] = keep[tile]
                give_ref[place] = give[tile]


def merge(core, grads, errors, prior):
    rows, columns = grads.shape
    rank = prior.shape[0]
    tiles = jax.ShapeDtypeStruct((rows // 128 * (rank // 32), 16, 128), jnp.float32)
    return pl.pallas_call(
        merge_kernel,
        in_specs=[SCALAR, ANYWHERE, ANYWHERE, ANYWHERE],
        out_specs=[WHOLE, WHOLE, WHOLE],
        out_shape=[pltpu.VMEM(grads.shape, jnp.bfloat16), tiles, tiles],
        scratch_shapes=[
            pltpu.VMEM(grads.shape, jnp.bfloat16),
            pltpu.VMEM(grads.shape, jnp.bfloat16),
            pltpu.VMEM(prior.shape, jnp.float32),
            pltpu.SemaphoreType.DMA((2, rows // MERGE_CHUNK)),
            pltpu.SemaphoreType.DMA,
        ],
        compiler_params=pltpu.CompilerParams(vmem_limit_bytes=VMEM_LIMIT),
        cost_estimate=pl.CostEstimate(
            flops=2 * rows * columns * rank, bytes_accessed=6 * rows * columns, transcendentals=0
        ),
    )(core, *[pltpu.with_memory_space_constraint(x, pltpu.HBM) for x in (grads, errors, prior)])


def inverse_factor(gram):
    rank = gram.shape[0]
    shape = (GROUP, 2 * rank)
    row = lax.broadcasted_iota(jnp.int32, (rank, rank), 0)
    column = lax.broadcasted_iota(jnp.int32, (rank, rank), 1)
    state = jnp.concatenate([gram, jnp.where(row == column, 1.0, 0.0)], axis=1)
    groups = [state[GROUP * g : GROUP * g + GROUP] for g in range(rank // GROUP)]
    place = lax.broadcasted_iota(jnp.int32, shape, 0)
    span = range(GROUP)
    for own in range(rank // GROUP):
        later = range(own, rank // GROUP)
        first = GROUP * own
        columns = [
            {g: jnp.broadcast_to(groups[g][:, first + j : first + j + 1], shape) for g in later}
            for j in span
        ]
        rows = [jnp.broadcast_to(groups[own][j : j + 1], shape) for j in span]
        cross = [
            [jnp.broadcast_to(columns[j][own][i : i + 1], shape) for j in range(i + 1)] for i in span
        ]
        for j in span:
            scale = lax.rsqrt(cross[j][j])
            rows[j] = rows[j] * scale
            for g in later:
                columns[j][g] = columns[j][g] * scale
            for i in range(j + 1, GROUP):
                cross[i][j] = cross[i][j] * scale
            for i in range(j + 1, GROUP):
                rows[i] = rows[i] - cross[i][j] * rows[j]
                for g in later:
                    columns[i][g] = columns[i][g] - columns[j][g] * cross[i][j]
                for l in range(j + 1, i + 1):
                    cross[i][l] = cross[i][l] - cross[i][j] * cross[l][j]
        for g in range(own + 1, rank // GROUP):
            for j in span:
                groups[g] = groups[g] - columns[j][g] * rows[j]
        groups[own] = rows[0]
        for j in range(1, GROUP):
            groups[own] = jnp.where(place == j, rows[j], groups[own])
    return jnp.concatenate(groups)[:, rank:]


def ortho_kernel(core_ref, half_ref, other_ref, merged_ref, ortho_ref, keep_ref, give_ref,
                 left_ref):
    core = core_ref[0]
    rank, rows = left_ref.shape
    across = rows // 128
    for place in range(half_ref.shape[0]):
        low, high = own_first(core, half_ref[place], other_ref[place])
        down = 16 * (place // across)
        lane = pl.ds(128 * (place % across), 128)
        left_ref[pl.ds(down, 16), lane] = low
        left_ref[pl.ds(rank // 2 + down, 16), lane] = high
    left = left_ref[...]
    gram = lax.dot_general(
        left, left, (((1,), (1,)), ((), ())), precision=lax.Precision.HIGHEST,
        preferred_element_type=jnp.float32,
    )
    ortho = jnp.dot(
        inverse_factor(gram), left, precision=lax.Precision.HIGHEST,
        preferred_element_type=jnp.float32,
    ).astype(jnp.bfloat16)
    ortho_ref[...] = ortho.T
    wide = keep_ref.shape[2]
    count = merged_ref.shape[1] // wide
    for lane in range(count):
        right = jnp.dot(
            ortho, merged_ref[:, wide * lane : wide * lane + wide],
            preferred_element_type=jnp.float32,
        )
        keep, give = own_first(core, right[: rank // 2], right[rank // 2 :])
        for down in range(rank // 16):
            keep_ref[down * count + lane] = keep[8 * down : 8 * down + 8]
            give_ref[down * count + lane] = give[8 * down : 8 * down + 8]


def orthonormal(core, half, other, merged, parts):
    rows, columns = merged.shape
    rank = half.size * 2 // rows
    wide = rank * columns // (8 * parts)
    tiles = jax.ShapeDtypeStruct((parts // 2, 8, wide), jnp.float32)
    return pl.pallas_call(
        ortho_kernel,
        in_specs=[SCALAR, WHOLE, WHOLE, WHOLE],
        out_specs=[WHOLE, WHOLE, WHOLE],
        out_shape=[pltpu.VMEM((rows, rank), jnp.bfloat16), tiles, tiles],
        scratch_shapes=[pltpu.VMEM((rank, rows), jnp.float32)],
        compiler_params=pltpu.CompilerParams(vmem_limit_bytes=VMEM_LIMIT),
        cost_estimate=pl.CostEstimate(
            flops=2 * rows * columns * rank, bytes_accessed=2 * rows * columns, transcendentals=0
        ),
    )(core, half, other, merged)


def finish_kernel(core_ref, slot_ref, half_ref, other_ref, ortho_ref, merged_ref,
                  update_ref, right_ref, errors_ref,
                  cast_ref, update_held, right_held, errors_held, small_sems, sems):
    core = core_ref[0]
    rank = ortho_ref.shape[1]
    own_rows = update_held.shape[0]
    wide = half_ref.shape[2]
    count = right_ref.shape[1] // wide
    for lane in range(count):
        pairs = [
            own_first(core, half_ref[down * count + lane], other_ref[down * count + lane])
            for down in range(rank // 16)
        ]
        right = jnp.concatenate([low for low, _ in pairs] + [high for _, high in pairs])
        cast_ref[:, wide * lane : wide * lane + wide] = right.astype(jnp.bfloat16)
        right_held[:, wide * lane : wide * lane + wide] = right
    cast = cast_ref[...]
    stores = []
    for i in range(merged_ref.shape[0] // FINISH_CHUNK):
        block = pl.ds(FINISH_CHUNK * i, FINISH_CHUNK)
        full_update = jnp.dot(ortho_ref[block], cast, preferred_element_type=jnp.float32)
        errors_held[block] = (
            merged_ref[block].astype(jnp.float32) - full_update
        ).astype(jnp.bfloat16)
        stores.append(
            pltpu.make_async_copy(errors_held.at[block], errors_ref.at[block], sems.at[i])
        )
        stores[-1].start()
        if i == 0:
            stores.append(pltpu.make_async_copy(right_held, right_ref, small_sems.at[0]))
            stores[-1].start()
            own = ortho_ref[pl.ds(pl.multiple_of(slot_ref[0] * own_rows, own_rows), own_rows)]
            update_held[...] = jnp.dot(
                own, cast, preferred_element_type=jnp.float32
            ).astype(jnp.bfloat16)
            stores.append(pltpu.make_async_copy(update_held, update_ref, small_sems.at[1]))
            stores[-1].start()
    for store in stores:
        store.wait()


def finish(core, slot, half, other, ortho, merged, parts):
    rows, columns = merged.shape
    rank = ortho.shape[1]
    small = (rows // parts, columns), (rank, columns)
    return pl.pallas_call(
        finish_kernel,
        in_specs=[SCALAR, SCALAR, WHOLE, WHOLE, WHOLE, WHOLE],
        out_specs=[ANYWHERE, ANYWHERE, ANYWHERE],
        out_shape=[
            pltpu.HBM(small[0], jnp.bfloat16),
            pltpu.HBM(small[1], jnp.float32),
            pltpu.HBM(merged.shape, jnp.bfloat16),
        ],
        scratch_shapes=[
            pltpu.VMEM(small[1], jnp.bfloat16),
            pltpu.VMEM(small[0], jnp.bfloat16),
            pltpu.VMEM(small[1], jnp.float32),
            pltpu.VMEM(merged.shape, jnp.bfloat16),
            pltpu.SemaphoreType.DMA((2,)),
            pltpu.SemaphoreType.DMA((rows // FINISH_CHUNK,)),
        ],
        compiler_params=pltpu.CompilerParams(vmem_limit_bytes=VMEM_LIMIT),
        cost_estimate=pl.CostEstimate(
            flops=2 * rows * columns * rank, bytes_accessed=4 * rows * columns, transcendentals=0
        ),
    )(core, slot, half, other, ortho, merged)


def swap_cores(value):
    return lax.ppermute(value, "core", [(0, 1), (1, 0)])


def exchange(value, axes):
    return lax.all_to_all(value, axes, 0, 0)


def added(parts):
    terms = [parts[i] for i in range(parts.shape[0])]
    while len(terms) > 1:
        terms = [a + b for a, b in zip(terms[::2], terms[1::2], strict=True)]
    return terms[0]


def spread(value, copies):
    return jnp.broadcast_to(value[None], (copies,) + value.shape)


def per_device(grads, errors, q_prev):
    core = lax.axis_index("core").astype(jnp.int32).reshape(1)
    slot = lax.axis_index(("y", "x", "core")).astype(jnp.int32).reshape(1)
    pairs = lax.axis_size("y") * lax.axis_size("x")
    depth = lax.axis_size("z")
    replicas = 2 * pairs

    core, slot, prior = lax.optimization_barrier((core, slot, q_prev.T))
    merged, keep, give = merge(core, grads[0], errors[0], prior)
    mine = added(exchange(keep + swap_cores(give), YX))
    mine = added(exchange(spread(mine, depth), "z")) / replicas
    half = exchange(spread(mine, pairs), YX)

    ortho, keep, give = orthonormal(core, half, swap_cores(half), merged, replicas)
    mine = added(exchange(keep + swap_cores(give), YX)) / replicas
    half = exchange(spread(mine, pairs), YX)

    update, right, new_errors = finish(
        core, slot, half, swap_cores(half), ortho, merged, replicas
    )
    return update, right.T, new_errors[None]


def solution(mesh):
    chips = Mesh(mesh.devices.reshape(4, 4, 2, 8), ("y", "x", "core", "z"))
    dp = ("y", "x", "core")
    placed = (P(dp, None, "z"), P(dp, None, "z"), P("z", None))
    return jax.shard_map(
        per_device,
        mesh=chips,
        in_specs=placed,
        out_specs=(P(dp, "z"), P("z", None), P(dp, None, "z")),
        check_vma=False,
    )
```

```python
import functools

import jax
import jax.numpy as jnp
from jax import lax
from jax.experimental import pallas as pl
from jax.experimental.pallas import tpu as pltpu
from jax.sharding import Mesh, PartitionSpec as P

YX = ("y", "x")
VMEM_LIMIT = 32 * 1024 * 1024
SMALL_LIMIT = 16 * 1024 * 1024
WHOLE = pl.BlockSpec(memory_space=pltpu.VMEM)
SCALAR = pl.BlockSpec(memory_space=pltpu.SMEM)
ANYWHERE = pl.BlockSpec(memory_space=pl.ANY)
MERGE_CHUNK = 512
FINISH_CHUNK = 128
GROUP = 8


def own_first(core, low, high):
    return jnp.where(core == 0, low, high), jnp.where(core == 0, high, low)


def merge_kernel(core_ref, grads_ref, errors_ref, prior_ref, merged_ref, keep_ref, give_ref,
                 grads_held, errors_held, prior_held, sems, prior_sem):
    core = core_ref[0]
    rank = prior_ref.shape[0]
    rows = merged_ref.shape[0]
    chunks = rows // MERGE_CHUNK
    prior_fetch = pltpu.make_async_copy(prior_ref, prior_held, prior_sem)
    prior_fetch.start()
    fetches = []
    for i in range(chunks):
        block = pl.ds(MERGE_CHUNK * i, MERGE_CHUNK)
        pair = (
            pltpu.make_async_copy(grads_ref.at[block], grads_held.at[block], sems.at[0, i]),
            pltpu.make_async_copy(errors_ref.at[block], errors_held.at[block], sems.at[1, i]),
        )
        for fetch in pair:
            fetch.start()
        fetches.append(pair)
    for i in range(chunks):
        block = pl.ds(MERGE_CHUNK * i, MERGE_CHUNK)
        for fetch in fetches[i]:
            fetch.wait()
        merged = (
            grads_held[block].astype(jnp.float32) + errors_held[block].astype(jnp.float32)
        ).astype(jnp.bfloat16)
        merged_ref[block] = merged
        if i == 0:
            prior_fetch.wait()
            prior = prior_held[...].astype(jnp.bfloat16)
        left = lax.dot_general(
            prior, merged, (((1,), (1,)), ((), ())), preferred_element_type=jnp.float32
        )
        keep, give = own_first(core, left[: rank // 2], left[rank // 2 :])
        lanes = MERGE_CHUNK // 128
        for down in range(rank // 32):
            for lane in range(lanes):
                place = down * (rows // 128) + i * lanes + lane
                tile = (slice(16 * down, 16 * down + 16), slice(128 * lane, 128 * lane + 128))
                keep_ref[place] = keep[tile]
                give_ref[place] = give[tile]


def merge(core, grads, errors, prior):
    rows, columns = grads.shape
    rank = prior.shape[0]
    tiles = jax.ShapeDtypeStruct((rows // 128 * (rank // 32), 16, 128), jnp.float32)
    return pl.pallas_call(
        merge_kernel,
        in_specs=[SCALAR, ANYWHERE, ANYWHERE, ANYWHERE],
        out_specs=[WHOLE, WHOLE, WHOLE],
        out_shape=[pltpu.VMEM(grads.shape, jnp.bfloat16), tiles, tiles],
        scratch_shapes=[
            pltpu.VMEM(grads.shape, jnp.bfloat16),
            pltpu.VMEM(grads.shape, jnp.bfloat16),
            pltpu.VMEM(prior.shape, jnp.float32),
            pltpu.SemaphoreType.DMA((2, rows // MERGE_CHUNK)),
            pltpu.SemaphoreType.DMA,
        ],
        compiler_params=pltpu.CompilerParams(vmem_limit_bytes=VMEM_LIMIT),
        cost_estimate=pl.CostEstimate(
            flops=2 * rows * columns * rank, bytes_accessed=6 * rows * columns, transcendentals=0
        ),
    )(core, *[pltpu.with_memory_space_constraint(x, pltpu.HBM) for x in (grads, errors, prior)])


def inverse_factor(gram):
    rank = gram.shape[0]
    shape = (GROUP, 2 * rank)
    row = lax.broadcasted_iota(jnp.int32, (rank, rank), 0)
    column = lax.broadcasted_iota(jnp.int32, (rank, rank), 1)
    state = jnp.concatenate([gram, jnp.where(row == column, 1.0, 0.0)], axis=1)
    groups = [state[GROUP * g : GROUP * g + GROUP] for g in range(rank // GROUP)]
    place = lax.broadcasted_iota(jnp.int32, shape, 0)
    span = range(GROUP)
    for own in range(rank // GROUP):
        later = range(own, rank // GROUP)
        first = GROUP * own
        columns = [
            {g: jnp.broadcast_to(groups[g][:, first + j : first + j + 1], shape) for g in later}
            for j in span
        ]
        rows = [jnp.broadcast_to(groups[own][j : j + 1], shape) for j in span]
        cross = [
            [jnp.broadcast_to(columns[j][own][i : i + 1], shape) for j in range(i + 1)] for i in span
        ]
        for j in span:
            scale = lax.rsqrt(cross[j][j])
            rows[j] = rows[j] * scale
            for g in later:
                columns[j][g] = columns[j][g] * scale
            for i in range(j + 1, GROUP):
                cross[i][j] = cross[i][j] * scale
            for i in range(j + 1, GROUP):
                rows[i] = rows[i] - cross[i][j] * rows[j]
                for g in later:
                    columns[i][g] = columns[i][g] - columns[j][g] * cross[i][j]
                for l in range(j + 1, i + 1):
                    cross[i][l] = cross[i][l] - cross[i][j] * cross[l][j]
        for g in range(own + 1, rank // GROUP):
            for j in span:
                groups[g] = groups[g] - columns[j][g] * rows[j]
        groups[own] = rows[0]
        for j in range(1, GROUP):
            groups[own] = jnp.where(place == j, rows[j], groups[own])
    return jnp.concatenate(groups)[:, rank:]


def right_tiles(ortho, merged_ref, half, tiles_ref):
    wide = tiles_ref.shape[2]
    count = merged_ref.shape[1] // (2 * wide)
    for lane in range(count):
        start = pl.multiple_of(half * (count * wide), 128) + lane * wide
        right = jnp.dot(
            ortho, merged_ref[:, pl.ds(start, wide)], preferred_element_type=jnp.float32
        )
        for down in range(ortho.shape[0] // 8):
            tiles_ref[down * count + lane] = right[8 * down : 8 * down + 8]


def ortho_kernel(core_ref, half_ref, other_ref, merged_ref, ortho_ref, give_ref, left_ref):
    core = core_ref[0]
    rank, rows = left_ref.shape
    across = rows // 128
    for place in range(half_ref.shape[0]):
        low, high = own_first(core, half_ref[place], other_ref[place])
        down = 16 * (place // across)
        lane = pl.ds(128 * (place % across), 128)
        left_ref[pl.ds(down, 16), lane] = low
        left_ref[pl.ds(rank // 2 + down, 16), lane] = high
    left = left_ref[...]
    gram = lax.dot_general(
        left, left, (((1,), (1,)), ((), ())), precision=lax.Precision.HIGHEST,
        preferred_element_type=jnp.float32,
    )
    ortho = jnp.dot(
        inverse_factor(gram), left, precision=lax.Precision.HIGHEST,
        preferred_element_type=jnp.float32,
    ).astype(jnp.bfloat16)
    ortho_ref[...] = ortho
    right_tiles(ortho, merged_ref, 1 - core, give_ref)


def keep_kernel(core_ref, ortho_ref, merged_ref, keep_ref, turned_ref):
    ortho = ortho_ref[...]
    right_tiles(ortho, merged_ref, core_ref[0], keep_ref)
    turned_ref[...] = ortho.T


def orthonormal(core, half, other, merged, parts):
    rows, columns = merged.shape
    rank = half.size * 2 // rows
    wide = rank * columns // (8 * parts)
    tiles = jax.ShapeDtypeStruct((parts // 2, 8, wide), jnp.float32)
    return pl.pallas_call(
        ortho_kernel,
        in_specs=[SCALAR, WHOLE, WHOLE, WHOLE],
        out_specs=[WHOLE, WHOLE],
        out_shape=[pltpu.VMEM((rank, rows), jnp.bfloat16), tiles],
        scratch_shapes=[pltpu.VMEM((rank, rows), jnp.float32)],
        compiler_params=pltpu.CompilerParams(vmem_limit_bytes=VMEM_LIMIT),
        cost_estimate=pl.CostEstimate(
            flops=2 * rows * columns * rank, bytes_accessed=2 * rows * columns, transcendentals=0
        ),
    )(core, half, other, merged)


def kept_right(core, ortho, merged, parts):
    rank, rows = ortho.shape
    columns = merged.shape[1]
    tiles = jax.ShapeDtypeStruct((parts // 2, 8, rank * columns // (8 * parts)), jnp.float32)
    return pl.pallas_call(
        keep_kernel,
        in_specs=[SCALAR, WHOLE, WHOLE],
        out_specs=[WHOLE, WHOLE],
        out_shape=[tiles, pltpu.VMEM((rows, rank), jnp.bfloat16)],
        compiler_params=pltpu.CompilerParams(vmem_limit_bytes=SMALL_LIMIT),
        cost_estimate=pl.CostEstimate(
            flops=rows * columns * rank, bytes_accessed=rows * columns, transcendentals=0
        ),
    )(core, ortho, merged)


def finish_kernel(flip, core_ref, slot_ref, tiles_ref, ortho_ref, merged_ref, *refs):
    update_ref, right_ref, errors_ref = refs[-9:-6]
    cast_ref, update_held, right_held, errors_held, small_sems, sems = refs[-6:]
    half = 1 - core_ref[0] if flip else core_ref[0]
    own_rows = update_held.shape[0]
    rank, columns = right_held.shape
    wide = tiles_ref.shape[2]
    count = columns // wide
    lanes = pl.ds(pl.multiple_of(half * columns, 128), columns)
    for lane in range(count):
        right = jnp.concatenate([tiles_ref[down * count + lane] for down in range(rank // 8)])
        cast_ref[:, wide * lane : wide * lane + wide] = right.astype(jnp.bfloat16)
        right_held[:, wide * lane : wide * lane + wide] = right
    cast = cast_ref[...]
    stores = []
    for i in range(merged_ref.shape[0] // FINISH_CHUNK):
        block = pl.ds(FINISH_CHUNK * i, FINISH_CHUNK)
        full_update = jnp.dot(ortho_ref[block], cast, preferred_element_type=jnp.float32)
        errors_held[block] = (
            merged_ref[block, lanes].astype(jnp.float32) - full_update
        ).astype(jnp.bfloat16)
        stores.append(
            pltpu.make_async_copy(errors_held.at[block], errors_ref.at[block, lanes], sems.at[i])
        )
        stores[-1].start()
        if i == 0:
            stores.append(
                pltpu.make_async_copy(right_held, right_ref.at[:, lanes], small_sems.at[0])
            )
            stores[-1].start()
            own = ortho_ref[pl.ds(pl.multiple_of(slot_ref[0] * own_rows, own_rows), own_rows)]
            update_held[...] = jnp.dot(
                own, cast, preferred_element_type=jnp.float32
            ).astype(jnp.bfloat16)
            stores.append(
                pltpu.make_async_copy(update_held, update_ref.at[:, lanes], small_sems.at[1])
            )
            stores[-1].start()
    for store in stores:
        store.wait()


def finish(core, slot, tiles, ortho, merged, parts, begun=()):
    rows, columns = merged.shape
    rank = ortho.shape[1]
    half = columns // 2
    return pl.pallas_call(
        functools.partial(finish_kernel, bool(begun)),
        in_specs=[SCALAR, SCALAR, WHOLE, WHOLE, WHOLE] + [ANYWHERE] * len(begun),
        out_specs=[ANYWHERE, ANYWHERE, ANYWHERE],
        out_shape=[
            pltpu.HBM((rows // parts, columns), jnp.bfloat16),
            pltpu.HBM((rank, columns), jnp.float32),
            pltpu.HBM(merged.shape, jnp.bfloat16),
        ],
        input_output_aliases={5 + i: i for i in range(len(begun))},
        scratch_shapes=[
            pltpu.VMEM((rank, half), jnp.bfloat16),
            pltpu.VMEM((rows // parts, half), jnp.bfloat16),
            pltpu.VMEM((rank, half), jnp.float32),
            pltpu.VMEM((rows, half), jnp.bfloat16),
            pltpu.SemaphoreType.DMA((2,)),
            pltpu.SemaphoreType.DMA((rows // FINISH_CHUNK,)),
        ],
        compiler_params=pltpu.CompilerParams(vmem_limit_bytes=SMALL_LIMIT),
        cost_estimate=pl.CostEstimate(
            flops=rows * columns * rank, bytes_accessed=2 * rows * columns, transcendentals=0
        ),
    )(core, slot, tiles, ortho, merged, *begun)


def swap_cores(value):
    return lax.ppermute(value, "core", [(0, 1), (1, 0)])


def exchange(value, axes):
    return lax.all_to_all(value, axes, 0, 0)


def added(parts):
    terms = [parts[i] for i in range(parts.shape[0])]
    while len(terms) > 1:
        terms = [a + b for a, b in zip(terms[::2], terms[1::2], strict=True)]
    return terms[0]


def spread(value, copies):
    return jnp.broadcast_to(value[None], (copies,) + value.shape)


def per_device(grads, errors, q_prev):
    core = lax.axis_index("core").astype(jnp.int32).reshape(1)
    slot = lax.axis_index(("y", "x", "core")).astype(jnp.int32).reshape(1)
    pairs = lax.axis_size("y") * lax.axis_size("x")
    depth = lax.axis_size("z")
    replicas = 2 * pairs

    core, slot, prior = lax.optimization_barrier((core, slot, q_prev.T))
    merged, keep, give = merge(core, grads[0], errors[0], prior)
    mine = added(exchange(keep + swap_cores(give), YX))
    mine = added(exchange(spread(mine, depth), "z")) / replicas
    half = exchange(spread(mine, pairs), YX)

    ortho, give = orthonormal(core, half, swap_cores(half), merged, replicas)
    given = swap_cores(give)
    keep, ortho = kept_right(core, ortho, merged, replicas)
    mine = added(exchange(keep + given, YX)) / replicas
    half = exchange(spread(mine, pairs), YX)

    other = swap_cores(half)
    begun = finish(core, slot, half, ortho, merged, replicas)
    update, right, new_errors = finish(core, slot, other, ortho, merged, replicas, begun)
    return update, right.T, new_errors[None]


def solution(mesh):
    chips = Mesh(mesh.devices.reshape(4, 4, 2, 8), ("y", "x", "core", "z"))
    dp = ("y", "x", "core")
    placed = (P(dp, None, "z"), P(dp, None, "z"), P("z", None))
    return jax.shard_map(
        per_device,
        mesh=chips,
        in_specs=placed,
        out_specs=(P(dp, "z"), P("z", None), P(dp, None, "z")),
        check_vma=False,
    )
```

```python
import functools

import jax
import jax.numpy as jnp
from jax import lax
from jax.experimental import pallas as pl
from jax.experimental.pallas import tpu as pltpu
from jax.sharding import Mesh, PartitionSpec as P

YX = ("y", "x")
DP = ("y", "x", "core")
VMEM_LIMIT = 32 * 1024 * 1024
SMALL_LIMIT = 16 * 1024 * 1024
WHOLE = pl.BlockSpec(memory_space=pltpu.VMEM)
SCALAR = pl.BlockSpec(memory_space=pltpu.SMEM)
ANYWHERE = pl.BlockSpec(memory_space=pl.ANY)
MERGE_CHUNK = 512
FINISH_CHUNK = 128
GROUP = 8


def merge_kernel(grads_ref, errors_ref, prior_ref, merged_ref, left_ref,
                 grads_held, errors_held, prior_held, sems, prior_sem):
    rank = prior_ref.shape[0]
    rows = merged_ref.shape[0]
    chunks = rows // MERGE_CHUNK
    prior_fetch = pltpu.make_async_copy(prior_ref, prior_held, prior_sem)
    prior_fetch.start()
    fetches = []
    for i in range(chunks):
        block = pl.ds(MERGE_CHUNK * i, MERGE_CHUNK)
        pair = (
            pltpu.make_async_copy(grads_ref.at[block], grads_held.at[block], sems.at[0, i]),
            pltpu.make_async_copy(errors_ref.at[block], errors_held.at[block], sems.at[1, i]),
        )
        for fetch in pair:
            fetch.start()
        fetches.append(pair)
    for i in range(chunks):
        block = pl.ds(MERGE_CHUNK * i, MERGE_CHUNK)
        for fetch in fetches[i]:
            fetch.wait()
        merged = (
            grads_held[block].astype(jnp.float32) + errors_held[block].astype(jnp.float32)
        ).astype(jnp.bfloat16)
        merged_ref[block] = merged
        if i == 0:
            prior_fetch.wait()
            prior = prior_held[...].astype(jnp.bfloat16)
        left = lax.dot_general(
            prior, merged, (((1,), (1,)), ((), ())), preferred_element_type=jnp.float32
        )
        lanes = MERGE_CHUNK // 128
        for down in range(rank // 16):
            for lane in range(lanes):
                left_ref[down * (rows // 128) + i * lanes + lane] = (
                    left[16 * down : 16 * down + 16, 128 * lane : 128 * lane + 128]
                )


def merge(grads, errors, prior):
    rows, columns = grads.shape
    rank = prior.shape[0]
    tiles = jax.ShapeDtypeStruct((rows // 128 * (rank // 16), 16, 128), jnp.float32)
    return pl.pallas_call(
        merge_kernel,
        in_specs=[ANYWHERE, ANYWHERE, ANYWHERE],
        out_specs=[WHOLE, WHOLE],
        out_shape=[pltpu.VMEM(grads.shape, jnp.bfloat16), tiles],
        scratch_shapes=[
            pltpu.VMEM(grads.shape, jnp.bfloat16),
            pltpu.VMEM(grads.shape, jnp.bfloat16),
            pltpu.VMEM(prior.shape, jnp.float32),
            pltpu.SemaphoreType.DMA((2, rows // MERGE_CHUNK)),
            pltpu.SemaphoreType.DMA,
        ],
        compiler_params=pltpu.CompilerParams(vmem_limit_bytes=VMEM_LIMIT),
        cost_estimate=pl.CostEstimate(
            flops=2 * rows * columns * rank, bytes_accessed=6 * rows * columns, transcendentals=0
        ),
    )(*[pltpu.with_memory_space_constraint(x, pltpu.HBM) for x in (grads, errors, prior)])


def inverse_factor(gram):
    rank = gram.shape[0]
    shape = (GROUP, 2 * rank)
    row = lax.broadcasted_iota(jnp.int32, (rank, rank), 0)
    column = lax.broadcasted_iota(jnp.int32, (rank, rank), 1)
    state = jnp.concatenate([gram, jnp.where(row == column, 1.0, 0.0)], axis=1)
    groups = [state[GROUP * g : GROUP * g + GROUP] for g in range(rank // GROUP)]
    place = lax.broadcasted_iota(jnp.int32, shape, 0)
    span = range(GROUP)
    for own in range(rank // GROUP):
        later = range(own, rank // GROUP)
        first = GROUP * own
        columns = [
            {g: jnp.broadcast_to(groups[g][:, first + j : first + j + 1], shape) for g in later}
            for j in span
        ]
        rows = [jnp.broadcast_to(groups[own][j : j + 1], shape) for j in span]
        cross = [
            [jnp.broadcast_to(columns[j][own][i : i + 1], shape) for j in range(i + 1)] for i in span
        ]
        for j in span:
            scale = lax.rsqrt(cross[j][j])
            rows[j] = rows[j] * scale
            for g in later:
                columns[j][g] = columns[j][g] * scale
            for i in range(j + 1, GROUP):
                cross[i][j] = cross[i][j] * scale
            for i in range(j + 1, GROUP):
                rows[i] = rows[i] - cross[i][j] * rows[j]
                for g in later:
                    columns[i][g] = columns[i][g] - columns[j][g] * cross[i][j]
                for l in range(j + 1, i + 1):
                    cross[i][l] = cross[i][l] - cross[i][j] * cross[l][j]
        for g in range(own + 1, rank // GROUP):
            for j in span:
                groups[g] = groups[g] - columns[j][g] * rows[j]
        groups[own] = rows[0]
        for j in range(1, GROUP):
            groups[own] = jnp.where(place == j, rows[j], groups[own])
    return jnp.concatenate(groups)[:, rank:]


def right_tiles(ortho, merged_ref, half, tiles_ref):
    wide = tiles_ref.shape[2]
    count = merged_ref.shape[1] // (2 * wide)
    for lane in range(count):
        start = pl.multiple_of(half * (count * wide), 128) + lane * wide
        right = jnp.dot(
            ortho, merged_ref[:, pl.ds(start, wide)], preferred_element_type=jnp.float32
        )
        for down in range(ortho.shape[0] // 8):
            tiles_ref[down * count + lane] = right[8 * down : 8 * down + 8]


def ortho_kernel(core_ref, tiles_ref, merged_ref, ortho_ref, give_ref, left_ref):
    core = core_ref[0]
    rank, rows = left_ref.shape
    across = rows // 128
    for place in range(tiles_ref.shape[0]):
        down, lane = divmod(place, across)
        left_ref[16 * down : 16 * down + 16, 128 * lane : 128 * lane + 128] = tiles_ref[place]
    left = left_ref[...]
    gram = lax.dot_general(
        left, left, (((1,), (1,)), ((), ())), precision=lax.Precision.HIGHEST,
        preferred_element_type=jnp.float32,
    )
    ortho = jnp.dot(
        inverse_factor(gram), left, precision=lax.Precision.HIGHEST,
        preferred_element_type=jnp.float32,
    ).astype(jnp.bfloat16)
    ortho_ref[...] = ortho
    right_tiles(ortho, merged_ref, 1 - core, give_ref)


def keep_kernel(core_ref, ortho_ref, merged_ref, keep_ref, turned_ref):
    ortho = ortho_ref[...]
    right_tiles(ortho, merged_ref, core_ref[0], keep_ref)
    turned_ref[...] = ortho.T


def orthonormal(core, left, merged, parts):
    rows, columns = merged.shape
    rank = left.size // rows
    wide = rank * columns // (8 * parts)
    tiles = jax.ShapeDtypeStruct((parts // 2, 8, wide), jnp.float32)
    return pl.pallas_call(
        ortho_kernel,
        in_specs=[SCALAR, WHOLE, WHOLE],
        out_specs=[WHOLE, WHOLE],
        out_shape=[pltpu.VMEM((rank, rows), jnp.bfloat16), tiles],
        scratch_shapes=[pltpu.VMEM((rank, rows), jnp.float32)],
        compiler_params=pltpu.CompilerParams(vmem_limit_bytes=VMEM_LIMIT),
        cost_estimate=pl.CostEstimate(
            flops=2 * rows * columns * rank, bytes_accessed=2 * rows * columns, transcendentals=0
        ),
    )(core, left, merged)


def kept_right(core, ortho, merged, parts):
    rank, rows = ortho.shape
    columns = merged.shape[1]
    tiles = jax.ShapeDtypeStruct((parts // 2, 8, rank * columns // (8 * parts)), jnp.float32)
    return pl.pallas_call(
        keep_kernel,
        in_specs=[SCALAR, WHOLE, WHOLE],
        out_specs=[WHOLE, WHOLE],
        out_shape=[tiles, pltpu.VMEM((rows, rank), jnp.bfloat16)],
        compiler_params=pltpu.CompilerParams(vmem_limit_bytes=SMALL_LIMIT),
        cost_estimate=pl.CostEstimate(
            flops=rows * columns * rank, bytes_accessed=rows * columns, transcendentals=0
        ),
    )(core, ortho, merged)


def finish_kernel(slot_ref, tiles_ref, ortho_ref, merged_ref, update_ref, right_ref, errors_ref,
                  cast_ref, update_held, right_held, errors_held, small_sems, sems):
    own_rows = update_held.shape[0]
    rank, columns = right_held.shape
    wide = tiles_ref.shape[2]
    count = columns // (2 * wide)
    for place in range(tiles_ref.shape[0]):
        spot, half = divmod(place, 2)
        down, lane = spot // count, half * count + spot % count
        right_held[8 * down : 8 * down + 8, wide * lane : wide * lane + wide] = (
            tiles_ref[place].astype(jnp.float32)
        )
    cast_ref[...] = right_held[...].astype(jnp.bfloat16)
    cast = cast_ref[...]
    stores = []
    for i in range(merged_ref.shape[0] // FINISH_CHUNK):
        block = pl.ds(FINISH_CHUNK * i, FINISH_CHUNK)
        full_update = jnp.dot(ortho_ref[block], cast, preferred_element_type=jnp.float32)
        errors_held[block] = (
            merged_ref[block].astype(jnp.float32) - full_update
        ).astype(jnp.bfloat16)
        stores.append(
            pltpu.make_async_copy(errors_held.at[block], errors_ref.at[block], sems.at[i])
        )
        stores[-1].start()
        if i == 0:
            stores.append(pltpu.make_async_copy(right_held, right_ref, small_sems.at[0]))
            stores[-1].start()
            own = ortho_ref[pl.ds(pl.multiple_of(slot_ref[0] * own_rows, own_rows), own_rows)]
            update_held[...] = jnp.dot(
                own, cast, preferred_element_type=jnp.float32
            ).astype(jnp.bfloat16)
            stores.append(pltpu.make_async_copy(update_held, update_ref, small_sems.at[1]))
            stores[-1].start()
    for store in stores:
        store.wait()


def finish(slot, tiles, ortho, merged, parts):
    rows, columns = merged.shape
    rank = ortho.shape[1]
    return pl.pallas_call(
        finish_kernel,
        in_specs=[SCALAR, WHOLE, WHOLE, WHOLE],
        out_specs=[ANYWHERE, ANYWHERE, ANYWHERE],
        out_shape=[
            pltpu.HBM((rows // parts, columns), jnp.bfloat16),
            pltpu.HBM((rank, columns), jnp.float32),
            pltpu.HBM(merged.shape, jnp.bfloat16),
        ],
        scratch_shapes=[
            pltpu.VMEM((rank, columns), jnp.bfloat16),
            pltpu.VMEM((rows // parts, columns), jnp.bfloat16),
            pltpu.VMEM((rank, columns), jnp.float32),
            pltpu.VMEM((rows, columns), jnp.bfloat16),
            pltpu.SemaphoreType.DMA((2,)),
            pltpu.SemaphoreType.DMA((rows // FINISH_CHUNK,)),
        ],
        compiler_params=pltpu.CompilerParams(vmem_limit_bytes=SMALL_LIMIT),
        cost_estimate=pl.CostEstimate(
            flops=2 * rows * columns * rank, bytes_accessed=4 * rows * columns, transcendentals=0
        ),
    )(slot, tiles, ortho, merged)


def swap_cores(value):
    return lax.ppermute(value, "core", [(0, 1), (1, 0)])


def exchange(value, axes):
    return lax.all_to_all(value, axes, 0, 0)


def added(parts):
    terms = [parts[i] for i in range(parts.shape[0])]
    while len(terms) > 1:
        terms = [a + b for a, b in zip(terms[::2], terms[1::2], strict=True)]
    return terms[0]


def spread(value, copies):
    return jnp.broadcast_to(value[None], (copies,) + value.shape)


def per_device(grads, errors, q_prev):
    core = lax.axis_index("core").astype(jnp.int32).reshape(1)
    slot = lax.axis_index(DP).astype(jnp.int32).reshape(1)
    pairs = lax.axis_size("y") * lax.axis_size("x")
    depth = lax.axis_size("z")
    replicas = 2 * pairs

    core, slot, prior = lax.optimization_barrier((core, slot, q_prev.T))
    merged, left = merge(grads[0], errors[0], prior)
    mine = added(exchange(left, DP))
    mine = added(exchange(spread(mine, depth), "z")) / replicas
    left = exchange(spread(mine, replicas), DP)

    ortho, give = orthonormal(core, left, merged, replicas)
    given = swap_cores(give)
    keep, ortho = kept_right(core, ortho, merged, replicas)
    mine = added(exchange(keep + given, YX)) / replicas
    right = exchange(spread(mine.astype(jnp.bfloat16), replicas), DP)
    update, right, new_errors = finish(slot, right, ortho, merged, replicas)
    return update, right.T, new_errors[None]


def solution(mesh):
    chips = Mesh(mesh.devices.reshape(4, 4, 2, 8), ("y", "x", "core", "z"))
    placed = (P(DP, None, "z"), P(DP, None, "z"), P("z", None))
    return jax.shard_map(
        per_device,
        mesh=chips,
        in_specs=placed,
        out_specs=(P(DP, "z"), P("z", None), P(DP, None, "z")),
        check_vma=False,
    )
```

```python
import functools

import jax
import jax.numpy as jnp
from jax import lax
from jax.experimental import pallas as pl
from jax.experimental.pallas import tpu as pltpu
from jax.sharding import Mesh, PartitionSpec as P

YX = ("y", "x")
DP = ("y", "x", "core")
VMEM_LIMIT = 32 * 1024 * 1024
SMALL_LIMIT = 16 * 1024 * 1024
WHOLE = pl.BlockSpec(memory_space=pltpu.VMEM)
ANYWHERE = pl.BlockSpec(memory_space=pl.ANY)
MERGE_CHUNK = 512
FINISH_CHUNK = 128
GROUP = 8


def merge_kernel(grads_ref, errors_ref, prior_ref, merged_ref, left_ref,
                 grads_held, errors_held, prior_held, sems, prior_sem):
    rank = prior_ref.shape[0]
    rows = merged_ref.shape[0]
    chunks = rows // MERGE_CHUNK
    prior_fetch = pltpu.make_async_copy(prior_ref, prior_held, prior_sem)
    prior_fetch.start()
    fetches = []
    for i in range(chunks):
        block = pl.ds(MERGE_CHUNK * i, MERGE_CHUNK)
        pair = (
            pltpu.make_async_copy(grads_ref.at[block], grads_held.at[block], sems.at[0, i]),
            pltpu.make_async_copy(errors_ref.at[block], errors_held.at[block], sems.at[1, i]),
        )
        for fetch in pair:
            fetch.start()
        fetches.append(pair)
    for i in range(chunks):
        block = pl.ds(MERGE_CHUNK * i, MERGE_CHUNK)
        for fetch in fetches[i]:
            fetch.wait()
        merged = (
            grads_held[block].astype(jnp.float32) + errors_held[block].astype(jnp.float32)
        ).astype(jnp.bfloat16)
        merged_ref[block] = merged
        if i == 0:
            prior_fetch.wait()
            prior = prior_held[...].astype(jnp.bfloat16)
        left = lax.dot_general(
            prior, merged, (((1,), (1,)), ((), ())), preferred_element_type=jnp.float32
        )
        lanes = MERGE_CHUNK // 128
        for down in range(rank // 16):
            for lane in range(lanes):
                left_ref[down * (rows // 128) + i * lanes + lane] = (
                    left[16 * down : 16 * down + 16, 128 * lane : 128 * lane + 128]
                )


def merge(grads, errors, prior):
    rows, columns = grads.shape
    rank = prior.shape[0]
    tiles = jax.ShapeDtypeStruct((rows // 128 * (rank // 16), 16, 128), jnp.float32)
    return pl.pallas_call(
        merge_kernel,
        in_specs=[ANYWHERE, ANYWHERE, ANYWHERE],
        out_specs=[WHOLE, WHOLE],
        out_shape=[pltpu.VMEM(grads.shape, jnp.bfloat16), tiles],
        scratch_shapes=[
            pltpu.VMEM(grads.shape, jnp.bfloat16),
            pltpu.VMEM(grads.shape, jnp.bfloat16),
            pltpu.VMEM(prior.shape, jnp.float32),
            pltpu.SemaphoreType.DMA((2, rows // MERGE_CHUNK)),
            pltpu.SemaphoreType.DMA,
        ],
        compiler_params=pltpu.CompilerParams(vmem_limit_bytes=VMEM_LIMIT),
        cost_estimate=pl.CostEstimate(
            flops=2 * rows * columns * rank, bytes_accessed=6 * rows * columns, transcendentals=0
        ),
    )(*[pltpu.with_memory_space_constraint(x, pltpu.HBM) for x in (grads, errors, prior)])


def inverse_factor(gram):
    rank = gram.shape[0]
    shape = (GROUP, 2 * rank)
    row = lax.broadcasted_iota(jnp.int32, (rank, rank), 0)
    column = lax.broadcasted_iota(jnp.int32, (rank, rank), 1)
    state = jnp.concatenate([gram, jnp.where(row == column, 1.0, 0.0)], axis=1)
    groups = [state[GROUP * g : GROUP * g + GROUP] for g in range(rank // GROUP)]
    place = lax.broadcasted_iota(jnp.int32, shape, 0)
    span = range(GROUP)
    for own in range(rank // GROUP):
        later = range(own, rank // GROUP)
        first = GROUP * own
        columns = [
            {g: jnp.broadcast_to(groups[g][:, first + j : first + j + 1], shape) for g in later}
            for j in span
        ]
        rows = [jnp.broadcast_to(groups[own][j : j + 1], shape) for j in span]
        cross = [
            [jnp.broadcast_to(columns[j][own][i : i + 1], shape) for j in range(i + 1)] for i in span
        ]
        for j in span:
            scale = lax.rsqrt(cross[j][j])
            rows[j] = rows[j] * scale
            for g in later:
                columns[j][g] = columns[j][g] * scale
            for i in range(j + 1, GROUP):
                cross[i][j] = cross[i][j] * scale
            for i in range(j + 1, GROUP):
                rows[i] = rows[i] - cross[i][j] * rows[j]
                for g in later:
                    columns[i][g] = columns[i][g] - columns[j][g] * cross[i][j]
                for l in range(j + 1, i + 1):
                    cross[i][l] = cross[i][l] - cross[i][j] * cross[l][j]
        for g in range(own + 1, rank // GROUP):
            for j in span:
                groups[g] = groups[g] - columns[j][g] * rows[j]
        groups[own] = rows[0]
        for j in range(1, GROUP):
            groups[own] = jnp.where(place == j, rows[j], groups[own])
        half = rank // GROUP // 2
        if (own + 1) % half == 0:
            yield jnp.concatenate(groups[own + 1 - half : own + 1])[:, rank:]


def right_tiles(ortho, merged_ref, half, tiles_ref):
    wide = tiles_ref.shape[2]
    count = merged_ref.shape[1] // (2 * wide)
    for lane in range(count):
        start = pl.multiple_of(half * (count * wide), 128) + lane * wide
        right = jnp.dot(
            ortho, merged_ref[:, pl.ds(start, wide)], preferred_element_type=jnp.float32
        )
        for down in range(ortho.shape[0] // 8):
            tiles_ref[down * count + lane] = right[8 * down : 8 * down + 8]


def ortho_kernel(tiles_ref, merged_ref, ortho_ref, give_ref, left_ref):
    rank, rows = left_ref.shape
    across = rows // 128
    for place in range(tiles_ref.shape[0]):
        down, lane = divmod(place, across)
        left_ref[16 * down : 16 * down + 16, 128 * lane : 128 * lane + 128] = tiles_ref[place]
    left = left_ref[...]
    gram = lax.dot_general(
        left, left, (((1,), (1,)), ((), ())), precision=lax.Precision.HIGHEST,
        preferred_element_type=jnp.float32,
    )
    ortho = jnp.concatenate([
        jnp.dot(
            inverse, left, precision=lax.Precision.HIGHEST, preferred_element_type=jnp.float32
        ).astype(jnp.bfloat16)
        for inverse in inverse_factor(gram)
    ])
    ortho_ref[...] = ortho
    right_tiles(ortho, merged_ref, 1 - lax.axis_index("core"), give_ref)


def keep_kernel(ortho_ref, merged_ref, keep_ref, turned_ref):
    ortho = ortho_ref[...]
    right_tiles(ortho, merged_ref, lax.axis_index("core"), keep_ref)
    turned_ref[...] = ortho.T


def orthonormal(left, merged, parts):
    rows, columns = merged.shape
    rank = left.size // rows
    wide = rank * columns // (8 * parts)
    tiles = jax.ShapeDtypeStruct((parts // 2, 8, wide), jnp.float32)
    return pl.pallas_call(
        ortho_kernel,
        in_specs=[WHOLE, WHOLE],
        out_specs=[WHOLE, WHOLE],
        out_shape=[pltpu.VMEM((rank, rows), jnp.bfloat16), tiles],
        scratch_shapes=[pltpu.VMEM((rank, rows), jnp.float32)],
        compiler_params=pltpu.CompilerParams(vmem_limit_bytes=VMEM_LIMIT),
        cost_estimate=pl.CostEstimate(
            flops=2 * rows * columns * rank, bytes_accessed=2 * rows * columns, transcendentals=0
        ),
    )(left, merged)


def kept_right(ortho, merged, parts):
    rank, rows = ortho.shape
    columns = merged.shape[1]
    tiles = jax.ShapeDtypeStruct((parts // 2, 8, rank * columns // (8 * parts)), jnp.float32)
    return pl.pallas_call(
        keep_kernel,
        in_specs=[WHOLE, WHOLE],
        out_specs=[WHOLE, WHOLE],
        out_shape=[tiles, pltpu.VMEM((rows, rank), jnp.bfloat16)],
        compiler_params=pltpu.CompilerParams(vmem_limit_bytes=SMALL_LIMIT),
        cost_estimate=pl.CostEstimate(
            flops=rows * columns * rank, bytes_accessed=rows * columns, transcendentals=0
        ),
    )(ortho, merged)


def finish_kernel(tiles_ref, ortho_ref, merged_ref, update_ref, right_ref, errors_ref,
                  cast_ref, update_held, right_held, errors_held, small_sems, sems):
    own_rows = update_held.shape[0]
    rank, columns = right_held.shape
    wide = tiles_ref.shape[2]
    count = columns // (2 * wide)
    for place in range(tiles_ref.shape[0]):
        spot, half = divmod(place, 2)
        down, lane = spot // count, half * count + spot % count
        right_held[8 * down : 8 * down + 8, wide * lane : wide * lane + wide] = (
            tiles_ref[place].astype(jnp.float32)
        )
    cast_ref[...] = right_held[...].astype(jnp.bfloat16)
    cast = cast_ref[...]
    stores = []
    for i in range(merged_ref.shape[0] // FINISH_CHUNK):
        block = pl.ds(FINISH_CHUNK * i, FINISH_CHUNK)
        full_update = jnp.dot(ortho_ref[block], cast, preferred_element_type=jnp.float32)
        errors_held[block] = (
            merged_ref[block].astype(jnp.float32) - full_update
        ).astype(jnp.bfloat16)
        stores.append(
            pltpu.make_async_copy(errors_held.at[block], errors_ref.at[block], sems.at[i])
        )
        stores[-1].start()
        if i == 0:
            stores.append(pltpu.make_async_copy(right_held, right_ref, small_sems.at[0]))
            stores[-1].start()
            own = ortho_ref[pl.ds(pl.multiple_of(lax.axis_index(DP) * own_rows, own_rows), own_rows)]
            update_held[...] = jnp.dot(
                own, cast, preferred_element_type=jnp.float32
            ).astype(jnp.bfloat16)
            stores.append(pltpu.make_async_copy(update_held, update_ref, small_sems.at[1]))
            stores[-1].start()
    for store in stores:
        store.wait()


def finish(tiles, ortho, merged, parts):
    rows, columns = merged.shape
    rank = ortho.shape[1]
    return pl.pallas_call(
        finish_kernel,
        in_specs=[WHOLE, WHOLE, WHOLE],
        out_specs=[ANYWHERE, ANYWHERE, ANYWHERE],
        out_shape=[
            pltpu.HBM((rows // parts, columns), jnp.bfloat16),
            pltpu.HBM((rank, columns), jnp.float32),
            pltpu.HBM(merged.shape, jnp.bfloat16),
        ],
        scratch_shapes=[
            pltpu.VMEM((rank, columns), jnp.bfloat16),
            pltpu.VMEM((rows // parts, columns), jnp.bfloat16),
            pltpu.VMEM((rank, columns), jnp.float32),
            pltpu.VMEM((rows, columns), jnp.bfloat16),
            pltpu.SemaphoreType.DMA((2,)),
            pltpu.SemaphoreType.DMA((rows // FINISH_CHUNK,)),
        ],
        compiler_params=pltpu.CompilerParams(vmem_limit_bytes=SMALL_LIMIT),
        cost_estimate=pl.CostEstimate(
            flops=2 * rows * columns * rank, bytes_accessed=4 * rows * columns, transcendentals=0
        ),
    )(tiles, ortho, merged)


def swap_cores(value):
    return lax.ppermute(value, "core", [(0, 1), (1, 0)])


def exchange(value, axes):
    return lax.all_to_all(value, axes, 0, 0)


def added(parts):
    terms = [parts[i] for i in range(parts.shape[0])]
    while len(terms) > 1:
        terms = [a + b for a, b in zip(terms[::2], terms[1::2], strict=True)]
    return terms[0]


def spread(value, copies):
    return jnp.broadcast_to(value[None], (copies,) + value.shape)


def per_device(grads, errors, q_prev):
    pairs = lax.axis_size("y") * lax.axis_size("x")
    depth = lax.axis_size("z")
    replicas = 2 * pairs

    merged, left = merge(grads[0], errors[0], q_prev.T)
    mine = added(exchange(left, DP))
    mine = added(exchange(spread(mine, depth), "z")) / replicas
    left = exchange(spread(mine, replicas), DP)

    ortho, give = orthonormal(left, merged, replicas)
    given = swap_cores(give)
    keep, ortho = kept_right(ortho, merged, replicas)
    mine = added(exchange(keep + given, YX)) / replicas
    right = exchange(spread(mine.astype(jnp.bfloat16), replicas), DP)
    update, right, new_errors = finish(right, ortho, merged, replicas)
    return update, right.T, new_errors[None]


def solution(mesh):
    chips = Mesh(mesh.devices.reshape(4, 4, 2, 8), ("y", "x", "core", "z"))
    placed = (P(DP, None, "z"), P(DP, None, "z"), P("z", None))
    return jax.shard_map(
        per_device,
        mesh=chips,
        in_specs=placed,
        out_specs=(P(DP, "z"), P("z", None), P(DP, None, "z")),
        check_vma=False,
    )
```

```python
import functools

import jax
import jax.numpy as jnp
from jax import lax
from jax.experimental import pallas as pl
from jax.experimental.pallas import tpu as pltpu
from jax.sharding import Mesh, PartitionSpec as P

YX = ("y", "x")
DP = ("y", "x", "core")
ALL = ("core", "y", "x")
VMEM_LIMIT = 32 * 1024 * 1024
SMALL_LIMIT = 16 * 1024 * 1024
WHOLE = pl.BlockSpec(memory_space=pltpu.VMEM)
ANYWHERE = pl.BlockSpec(memory_space=pl.ANY)
MERGE_CHUNK = 512
FINISH_CHUNK = 128
GROUP = 8


def merge_kernel(grads_ref, errors_ref, prior_ref, merged_ref, left_ref,
                 grads_held, errors_held, prior_held, sems, prior_sem):
    rank = prior_ref.shape[0]
    rows = merged_ref.shape[0]
    chunks = rows // MERGE_CHUNK
    prior_fetch = pltpu.make_async_copy(prior_ref, prior_held, prior_sem)
    prior_fetch.start()
    fetches = []
    for i in range(chunks):
        block = pl.ds(MERGE_CHUNK * i, MERGE_CHUNK)
        pair = (
            pltpu.make_async_copy(grads_ref.at[block], grads_held.at[block], sems.at[0, i]),
            pltpu.make_async_copy(errors_ref.at[block], errors_held.at[block], sems.at[1, i]),
        )
        for fetch in pair:
            fetch.start()
        fetches.append(pair)
    for i in range(chunks):
        block = pl.ds(MERGE_CHUNK * i, MERGE_CHUNK)
        for fetch in fetches[i]:
            fetch.wait()
        merged = (
            grads_held[block].astype(jnp.float32) + errors_held[block].astype(jnp.float32)
        ).astype(jnp.bfloat16)
        merged_ref[block] = merged
        if i == 0:
            prior_fetch.wait()
            prior = prior_held[...].astype(jnp.bfloat16)
        left = lax.dot_general(
            prior, merged, (((1,), (1,)), ((), ())), preferred_element_type=jnp.float32
        )
        lanes = MERGE_CHUNK // 128
        for down in range(rank // 16):
            for lane in range(lanes):
                left_ref[down * (rows // 128) + i * lanes + lane] = (
                    left[16 * down : 16 * down + 16, 128 * lane : 128 * lane + 128]
                )


def merge(grads, errors, prior):
    rows, columns = grads.shape
    rank = prior.shape[0]
    tiles = jax.ShapeDtypeStruct((rows // 128 * (rank // 16), 16, 128), jnp.float32)
    return pl.pallas_call(
        merge_kernel,
        in_specs=[ANYWHERE, ANYWHERE, ANYWHERE],
        out_specs=[WHOLE, WHOLE],
        out_shape=[pltpu.VMEM(grads.shape, jnp.bfloat16), tiles],
        scratch_shapes=[
            pltpu.VMEM(grads.shape, jnp.bfloat16),
            pltpu.VMEM(grads.shape, jnp.bfloat16),
            pltpu.VMEM(prior.shape, jnp.float32),
            pltpu.SemaphoreType.DMA((2, rows // MERGE_CHUNK)),
            pltpu.SemaphoreType.DMA,
        ],
        compiler_params=pltpu.CompilerParams(vmem_limit_bytes=VMEM_LIMIT),
        cost_estimate=pl.CostEstimate(
            flops=2 * rows * columns * rank, bytes_accessed=6 * rows * columns, transcendentals=0
        ),
    )(*[pltpu.with_memory_space_constraint(x, pltpu.HBM) for x in (grads, errors, prior)])


def inverse_factor(gram):
    rank = gram.shape[0]
    shape = (GROUP, 2 * rank)
    row = lax.broadcasted_iota(jnp.int32, (rank, rank), 0)
    column = lax.broadcasted_iota(jnp.int32, (rank, rank), 1)
    state = jnp.concatenate([gram, jnp.where(row == column, 1.0, 0.0)], axis=1)
    groups = [state[GROUP * g : GROUP * g + GROUP] for g in range(rank // GROUP)]
    place = lax.broadcasted_iota(jnp.int32, shape, 0)
    span = range(GROUP)
    for own in range(rank // GROUP):
        later = range(own, rank // GROUP)
        first = GROUP * own
        columns = [
            {g: jnp.broadcast_to(groups[g][:, first + j : first + j + 1], shape) for g in later}
            for j in span
        ]
        rows = [jnp.broadcast_to(groups[own][j : j + 1], shape) for j in span]
        cross = [
            [jnp.broadcast_to(columns[j][own][i : i + 1], shape) for j in range(i + 1)] for i in span
        ]
        for j in span:
            scale = lax.rsqrt(cross[j][j])
            rows[j] = rows[j] * scale
            for g in later:
                columns[j][g] = columns[j][g] * scale
            for i in range(j + 1, GROUP):
                cross[i][j] = cross[i][j] * scale
            for i in range(j + 1, GROUP):
                rows[i] = rows[i] - cross[i][j] * rows[j]
                for g in later:
                    columns[i][g] = columns[i][g] - columns[j][g] * cross[i][j]
                for l in range(j + 1, i + 1):
                    cross[i][l] = cross[i][l] - cross[i][j] * cross[l][j]
        for g in range(own + 1, rank // GROUP):
            for j in span:
                groups[g] = groups[g] - columns[j][g] * rows[j]
        groups[own] = rows[0]
        for j in range(1, GROUP):
            groups[own] = jnp.where(place == j, rows[j], groups[own])
        half = rank // GROUP // 2
        if (own + 1) % half == 0:
            yield jnp.concatenate(groups[own + 1 - half : own + 1])[:, rank:]


def right_tiles(ortho, merged_ref, half, tiles_ref):
    wide = tiles_ref.shape[2]
    count = merged_ref.shape[1] // (2 * wide)
    for lane in range(count):
        start = pl.multiple_of(half * (count * wide), 128) + lane * wide
        right = jnp.dot(
            ortho, merged_ref[:, pl.ds(start, wide)], preferred_element_type=jnp.float32
        )
        for down in range(ortho.shape[0] // 8):
            tiles_ref[down * count + lane] = right[8 * down : 8 * down + 8]


def ortho_kernel(tiles_ref, merged_ref, ortho_ref, give_ref, left_ref):
    rank, rows = left_ref.shape
    across = rows // 128
    for place in range(tiles_ref.shape[0]):
        down, lane = divmod(place, across)
        left_ref[16 * down : 16 * down + 16, 128 * lane : 128 * lane + 128] = tiles_ref[place]
    left = left_ref[...]
    gram = lax.dot_general(
        left, left, (((1,), (1,)), ((), ())), precision=lax.Precision.HIGHEST,
        preferred_element_type=jnp.float32,
    )
    ortho = jnp.concatenate([
        jnp.dot(
            inverse, left, precision=lax.Precision.HIGHEST, preferred_element_type=jnp.float32
        ).astype(jnp.bfloat16)
        for inverse in inverse_factor(gram)
    ])
    ortho_ref[...] = ortho
    right_tiles(ortho, merged_ref, 1 - lax.axis_index("core"), give_ref)


def keep_kernel(ortho_ref, merged_ref, keep_ref, turned_ref):
    ortho = ortho_ref[...]
    right_tiles(ortho, merged_ref, lax.axis_index("core"), keep_ref)
    turned_ref[...] = ortho.T


def orthonormal(left, merged, parts):
    rows, columns = merged.shape
    rank = left.size // rows
    wide = rank * columns // (8 * parts)
    tiles = jax.ShapeDtypeStruct((parts // 2, 8, wide), jnp.float32)
    return pl.pallas_call(
        ortho_kernel,
        in_specs=[WHOLE, WHOLE],
        out_specs=[WHOLE, WHOLE],
        out_shape=[pltpu.VMEM((rank, rows), jnp.bfloat16), tiles],
        scratch_shapes=[pltpu.VMEM((rank, rows), jnp.float32)],
        compiler_params=pltpu.CompilerParams(vmem_limit_bytes=VMEM_LIMIT),
        cost_estimate=pl.CostEstimate(
            flops=2 * rows * columns * rank, bytes_accessed=2 * rows * columns, transcendentals=0
        ),
    )(left, merged)


def kept_right(ortho, merged, parts):
    rank, rows = ortho.shape
    columns = merged.shape[1]
    tiles = jax.ShapeDtypeStruct((parts // 2, 8, rank * columns // (8 * parts)), jnp.float32)
    return pl.pallas_call(
        keep_kernel,
        in_specs=[WHOLE, WHOLE],
        out_specs=[WHOLE, WHOLE],
        out_shape=[tiles, pltpu.VMEM((rows, rank), jnp.bfloat16)],
        compiler_params=pltpu.CompilerParams(vmem_limit_bytes=SMALL_LIMIT),
        cost_estimate=pl.CostEstimate(
            flops=rows * columns * rank, bytes_accessed=rows * columns, transcendentals=0
        ),
    )(ortho, merged)


def finish_kernel(tiles_ref, ortho_ref, merged_ref, update_ref, right_ref, errors_ref,
                  cast_ref, update_held, right_held, errors_held, small_sems, sems):
    own_rows = update_held.shape[0]
    rank, columns = right_held.shape
    wide = tiles_ref.shape[2]
    count = columns // (2 * wide)
    for place in range(tiles_ref.shape[0]):
        half, spot = divmod(place, tiles_ref.shape[0] // 2)
        down, lane = spot // count, half * count + spot % count
        right_held[8 * down : 8 * down + 8, wide * lane : wide * lane + wide] = (
            tiles_ref[place].astype(jnp.float32)
        )
    cast_ref[...] = right_held[...].astype(jnp.bfloat16)
    cast = cast_ref[...]
    stores = []
    for i in range(merged_ref.shape[0] // FINISH_CHUNK):
        block = pl.ds(FINISH_CHUNK * i, FINISH_CHUNK)
        full_update = jnp.dot(ortho_ref[block], cast, preferred_element_type=jnp.float32)
        errors_held[block] = (
            merged_ref[block].astype(jnp.float32) - full_update
        ).astype(jnp.bfloat16)
        stores.append(
            pltpu.make_async_copy(errors_held.at[block], errors_ref.at[block], sems.at[i])
        )
        stores[-1].start()
        if i == 0:
            stores.append(pltpu.make_async_copy(right_held, right_ref, small_sems.at[0]))
            stores[-1].start()
            own = ortho_ref[pl.ds(pl.multiple_of(lax.axis_index(DP) * own_rows, own_rows), own_rows)]
            update_held[...] = jnp.dot(
                own, cast, preferred_element_type=jnp.float32
            ).astype(jnp.bfloat16)
            stores.append(pltpu.make_async_copy(update_held, update_ref, small_sems.at[1]))
            stores[-1].start()
    for store in stores:
        store.wait()


def finish(tiles, ortho, merged, parts):
    rows, columns = merged.shape
    rank = ortho.shape[1]
    return pl.pallas_call(
        finish_kernel,
        in_specs=[WHOLE, WHOLE, WHOLE],
        out_specs=[ANYWHERE, ANYWHERE, ANYWHERE],
        out_shape=[
            pltpu.HBM((rows // parts, columns), jnp.bfloat16),
            pltpu.HBM((rank, columns), jnp.float32),
            pltpu.HBM(merged.shape, jnp.bfloat16),
        ],
        scratch_shapes=[
            pltpu.VMEM((rank, columns), jnp.bfloat16),
            pltpu.VMEM((rows // parts, columns), jnp.bfloat16),
            pltpu.VMEM((rank, columns), jnp.float32),
            pltpu.VMEM((rows, columns), jnp.bfloat16),
            pltpu.SemaphoreType.DMA((2,)),
            pltpu.SemaphoreType.DMA((rows // FINISH_CHUNK,)),
        ],
        compiler_params=pltpu.CompilerParams(vmem_limit_bytes=SMALL_LIMIT),
        cost_estimate=pl.CostEstimate(
            flops=2 * rows * columns * rank, bytes_accessed=4 * rows * columns, transcendentals=0
        ),
    )(tiles, ortho, merged)


def swap_cores(value):
    return lax.ppermute(value, "core", [(0, 1), (1, 0)])


def exchange(value, axes):
    return lax.all_to_all(value, axes, 0, 0)


def added(parts):
    terms = [parts[i] for i in range(parts.shape[0])]
    while len(terms) > 1:
        terms = [a + b for a, b in zip(terms[::2], terms[1::2], strict=True)]
    return terms[0]


def spread(value, copies):
    return jnp.broadcast_to(value[None], (copies,) + value.shape)


def per_device(grads, errors, q_prev):
    pairs = lax.axis_size("y") * lax.axis_size("x")
    depth = lax.axis_size("z")
    replicas = 2 * pairs

    merged, left = merge(grads[0], errors[0], q_prev.T)
    mine = added(exchange(left, ALL))
    mine = added(exchange(spread(mine, depth), "z")) / replicas
    left = exchange(spread(mine, replicas), ALL)

    ortho, give = orthonormal(left, merged, replicas)
    given = swap_cores(give)
    keep, ortho = kept_right(ortho, merged, replicas)
    mine = added(exchange(keep + given, YX)) / replicas
    right = exchange(spread(mine.astype(jnp.bfloat16), replicas), ALL)
    update, right, new_errors = finish(right, ortho, merged, replicas)
    return update, right.T, new_errors[None]


def solution(mesh):
    chips = Mesh(mesh.devices.reshape(4, 4, 2, 8), ("y", "x", "core", "z"))
    placed = (P(DP, None, "z"), P(DP, None, "z"), P("z", None))
    return jax.shard_map(
        per_device,
        mesh=chips,
        in_specs=placed,
        out_specs=(P(DP, "z"), P("z", None), P(DP, None, "z")),
        check_vma=False,
    )
```

```python
import functools

import jax
import jax.numpy as jnp
from jax import lax
from jax.experimental import pallas as pl
from jax.experimental.pallas import tpu as pltpu
from jax.sharding import Mesh, PartitionSpec as P

YX = ("y", "x")
DP = ("y", "x", "core")
ALL = ("core", "y", "x")
VMEM_LIMIT = 32 * 1024 * 1024
SMALL_LIMIT = 16 * 1024 * 1024
WHOLE = pl.BlockSpec(memory_space=pltpu.VMEM)
ANYWHERE = pl.BlockSpec(memory_space=pl.ANY)
MERGE_CHUNK = 512
FINISH_CHUNK = 128
GROUP = 8


def merge_kernel(grads_ref, errors_ref, prior_ref, merged_ref, left_ref,
                 grads_held, errors_held, prior_held, sems, prior_sem):
    rank = prior_ref.shape[0]
    rows = merged_ref.shape[0]
    chunks = rows // MERGE_CHUNK
    prior_fetch = pltpu.make_async_copy(prior_ref, prior_held, prior_sem)
    prior_fetch.start()
    fetches = []
    for i in range(chunks):
        block = pl.ds(MERGE_CHUNK * i, MERGE_CHUNK)
        pair = (
            pltpu.make_async_copy(grads_ref.at[block], grads_held.at[block], sems.at[0, i]),
            pltpu.make_async_copy(errors_ref.at[block], errors_held.at[block], sems.at[1, i]),
        )
        for fetch in pair:
            fetch.start()
        fetches.append(pair)
    for i in range(chunks):
        block = pl.ds(MERGE_CHUNK * i, MERGE_CHUNK)
        for fetch in fetches[i]:
            fetch.wait()
        merged = (
            grads_held[block].astype(jnp.float32) + errors_held[block].astype(jnp.float32)
        ).astype(jnp.bfloat16)
        merged_ref[block] = merged
        if i == 0:
            prior_fetch.wait()
            prior = prior_held[...].astype(jnp.bfloat16)
        left = lax.dot_general(
            prior, merged, (((1,), (1,)), ((), ())), preferred_element_type=jnp.float32
        )
        lanes = MERGE_CHUNK // 128
        for down in range(rank // 16):
            for lane in range(lanes):
                left_ref[down * (rows // 128) + i * lanes + lane] = (
                    left[16 * down : 16 * down + 16, 128 * lane : 128 * lane + 128]
                )


def merge(grads, errors, prior):
    rows, columns = grads.shape
    rank = prior.shape[0]
    tiles = jax.ShapeDtypeStruct((rows // 128 * (rank // 16), 16, 128), jnp.float32)
    return pl.pallas_call(
        merge_kernel,
        in_specs=[ANYWHERE, ANYWHERE, ANYWHERE],
        out_specs=[WHOLE, WHOLE],
        out_shape=[pltpu.VMEM(grads.shape, jnp.bfloat16), tiles],
        scratch_shapes=[
            pltpu.VMEM(grads.shape, jnp.bfloat16),
            pltpu.VMEM(grads.shape, jnp.bfloat16),
            pltpu.VMEM(prior.shape, jnp.float32),
            pltpu.SemaphoreType.DMA((2, rows // MERGE_CHUNK)),
            pltpu.SemaphoreType.DMA,
        ],
        compiler_params=pltpu.CompilerParams(vmem_limit_bytes=VMEM_LIMIT),
        cost_estimate=pl.CostEstimate(
            flops=2 * rows * columns * rank, bytes_accessed=6 * rows * columns, transcendentals=0
        ),
    )(*[pltpu.with_memory_space_constraint(x, pltpu.HBM) for x in (grads, errors, prior)])


def inverse_factor(gram):
    rank = gram.shape[0]
    shape = (GROUP, 2 * rank)
    row = lax.broadcasted_iota(jnp.int32, (rank, rank), 0)
    column = lax.broadcasted_iota(jnp.int32, (rank, rank), 1)
    state = jnp.concatenate([gram, jnp.where(row == column, 1.0, 0.0)], axis=1)
    groups = [state[GROUP * g : GROUP * g + GROUP] for g in range(rank // GROUP)]
    place = lax.broadcasted_iota(jnp.int32, shape, 0)
    span = range(GROUP)
    for own in range(rank // GROUP):
        later = range(own, rank // GROUP)
        first = GROUP * own
        columns = [
            {g: jnp.broadcast_to(groups[g][:, first + j : first + j + 1], shape) for g in later}
            for j in span
        ]
        rows = [jnp.broadcast_to(groups[own][j : j + 1], shape) for j in span]
        cross = [
            [jnp.broadcast_to(columns[j][own][i : i + 1], shape) for j in range(i + 1)] for i in span
        ]
        for j in span:
            scale = lax.rsqrt(cross[j][j])
            rows[j] = rows[j] * scale
            for g in later:
                columns[j][g] = columns[j][g] * scale
            for i in range(j + 1, GROUP):
                cross[i][j] = cross[i][j] * scale
            for i in range(j + 1, GROUP):
                rows[i] = rows[i] - cross[i][j] * rows[j]
                for g in later:
                    columns[i][g] = columns[i][g] - columns[j][g] * cross[i][j]
                for l in range(j + 1, i + 1):
                    cross[i][l] = cross[i][l] - cross[i][j] * cross[l][j]
        for g in range(own + 1, rank // GROUP):
            for j in span:
                groups[g] = groups[g] - columns[j][g] * rows[j]
        groups[own] = rows[0]
        for j in range(1, GROUP):
            groups[own] = jnp.where(place == j, rows[j], groups[own])
        part = rank // GROUP // 4
        if (own + 1) % part == 0:
            yield jnp.concatenate(groups[own + 1 - part : own + 1])[:, rank:]


def right_tiles(ortho, merged_ref, half, tiles_ref):
    wide = tiles_ref.shape[2]
    count = merged_ref.shape[1] // (2 * wide)
    for lane in range(count):
        start = pl.multiple_of(half * (count * wide), 128) + lane * wide
        right = jnp.dot(
            ortho, merged_ref[:, pl.ds(start, wide)], preferred_element_type=jnp.float32
        )
        for down in range(ortho.shape[0] // 8):
            tiles_ref[down * count + lane] = right[8 * down : 8 * down + 8]


def ortho_kernel(tiles_ref, merged_ref, ortho_ref, give_ref, left_ref):
    rank, rows = left_ref.shape
    across = rows // 128
    for place in range(tiles_ref.shape[0]):
        down, lane = divmod(place, across)
        left_ref[16 * down : 16 * down + 16, 128 * lane : 128 * lane + 128] = tiles_ref[place]
    left = left_ref[...]
    gram = lax.dot_general(
        left, left, (((1,), (1,)), ((), ())), precision=lax.Precision.HIGHEST,
        preferred_element_type=jnp.float32,
    )
    ortho = jnp.concatenate([
        jnp.dot(
            inverse, left, precision=lax.Precision.HIGHEST, preferred_element_type=jnp.float32
        ).astype(jnp.bfloat16)
        for inverse in inverse_factor(gram)
    ])
    ortho_ref[...] = ortho
    right_tiles(ortho, merged_ref, 1 - lax.axis_index("core"), give_ref)


def keep_kernel(ortho_ref, merged_ref, keep_ref, turned_ref):
    ortho = ortho_ref[...]
    right_tiles(ortho, merged_ref, lax.axis_index("core"), keep_ref)
    turned_ref[...] = ortho.T


def orthonormal(left, merged, parts):
    rows, columns = merged.shape
    rank = left.size // rows
    wide = rank * columns // (8 * parts)
    tiles = jax.ShapeDtypeStruct((parts // 2, 8, wide), jnp.float32)
    return pl.pallas_call(
        ortho_kernel,
        in_specs=[WHOLE, WHOLE],
        out_specs=[WHOLE, WHOLE],
        out_shape=[pltpu.VMEM((rank, rows), jnp.bfloat16), tiles],
        scratch_shapes=[pltpu.VMEM((rank, rows), jnp.float32)],
        compiler_params=pltpu.CompilerParams(vmem_limit_bytes=VMEM_LIMIT),
        cost_estimate=pl.CostEstimate(
            flops=2 * rows * columns * rank, bytes_accessed=2 * rows * columns, transcendentals=0
        ),
    )(left, merged)


def kept_right(ortho, merged, parts):
    rank, rows = ortho.shape
    columns = merged.shape[1]
    tiles = jax.ShapeDtypeStruct((parts // 2, 8, rank * columns // (8 * parts)), jnp.float32)
    return pl.pallas_call(
        keep_kernel,
        in_specs=[WHOLE, WHOLE],
        out_specs=[WHOLE, WHOLE],
        out_shape=[tiles, pltpu.VMEM((rows, rank), jnp.bfloat16)],
        compiler_params=pltpu.CompilerParams(vmem_limit_bytes=SMALL_LIMIT),
        cost_estimate=pl.CostEstimate(
            flops=rows * columns * rank, bytes_accessed=rows * columns, transcendentals=0
        ),
    )(ortho, merged)


def finish_kernel(tiles_ref, ortho_ref, merged_ref, update_ref, right_ref, errors_ref,
                  cast_ref, update_held, right_held, errors_held, small_sems, sems):
    own_rows = update_held.shape[0]
    rank, columns = right_held.shape
    wide = tiles_ref.shape[2]
    count = columns // (2 * wide)
    for place in range(tiles_ref.shape[0]):
        half, spot = divmod(place, tiles_ref.shape[0] // 2)
        down, lane = spot // count, half * count + spot % count
        right_held[8 * down : 8 * down + 8, wide * lane : wide * lane + wide] = (
            tiles_ref[place].astype(jnp.float32)
        )
    cast_ref[...] = right_held[...].astype(jnp.bfloat16)
    cast = cast_ref[...]
    stores = []
    for i in range(merged_ref.shape[0] // FINISH_CHUNK):
        block = pl.ds(FINISH_CHUNK * i, FINISH_CHUNK)
        full_update = jnp.dot(ortho_ref[block], cast, preferred_element_type=jnp.float32)
        errors_held[block] = (
            merged_ref[block].astype(jnp.float32) - full_update
        ).astype(jnp.bfloat16)
        stores.append(
            pltpu.make_async_copy(errors_held.at[block], errors_ref.at[block], sems.at[i])
        )
        stores[-1].start()
        if i == 0:
            stores.append(pltpu.make_async_copy(right_held, right_ref, small_sems.at[0]))
            stores[-1].start()
            own = ortho_ref[pl.ds(pl.multiple_of(lax.axis_index(DP) * own_rows, own_rows), own_rows)]
            update_held[...] = jnp.dot(
                own, cast, preferred_element_type=jnp.float32
            ).astype(jnp.bfloat16)
            stores.append(pltpu.make_async_copy(update_held, update_ref, small_sems.at[1]))
            stores[-1].start()
    for store in stores:
        store.wait()


def finish(tiles, ortho, merged, parts):
    rows, columns = merged.shape
    rank = ortho.shape[1]
    return pl.pallas_call(
        finish_kernel,
        in_specs=[WHOLE, WHOLE, WHOLE],
        out_specs=[ANYWHERE, ANYWHERE, ANYWHERE],
        out_shape=[
            pltpu.HBM((rows // parts, columns), jnp.bfloat16),
            pltpu.HBM((rank, columns), jnp.float32),
            pltpu.HBM(merged.shape, jnp.bfloat16),
        ],
        scratch_shapes=[
            pltpu.VMEM((rank, columns), jnp.bfloat16),
            pltpu.VMEM((rows // parts, columns), jnp.bfloat16),
            pltpu.VMEM((rank, columns), jnp.float32),
            pltpu.VMEM((rows, columns), jnp.bfloat16),
            pltpu.SemaphoreType.DMA((2,)),
            pltpu.SemaphoreType.DMA((rows // FINISH_CHUNK,)),
        ],
        compiler_params=pltpu.CompilerParams(vmem_limit_bytes=SMALL_LIMIT),
        cost_estimate=pl.CostEstimate(
            flops=2 * rows * columns * rank, bytes_accessed=4 * rows * columns, transcendentals=0
        ),
    )(tiles, ortho, merged)


def swap_cores(value):
    return lax.ppermute(value, "core", [(0, 1), (1, 0)])


def exchange(value, axes):
    return lax.all_to_all(value, axes, 0, 0)


def added(parts):
    terms = [parts[i] for i in range(parts.shape[0])]
    while len(terms) > 1:
        terms = [a + b for a, b in zip(terms[::2], terms[1::2], strict=True)]
    return terms[0]


def spread(value, copies):
    return jnp.broadcast_to(value[None], (copies,) + value.shape)


def per_device(grads, errors, q_prev):
    pairs = lax.axis_size("y") * lax.axis_size("x")
    depth = lax.axis_size("z")
    replicas = 2 * pairs

    merged, left = merge(grads[0], errors[0], q_prev.T)
    mine = added(exchange(left, ALL))
    mine = added(exchange(spread(mine, depth), "z")) / replicas
    left = exchange(spread(mine, replicas), ALL)

    ortho, give = orthonormal(left, merged, replicas)
    given = swap_cores(give)
    keep, ortho = kept_right(ortho, merged, replicas)
    mine = added(exchange(keep + given, YX)) / replicas
    right = exchange(spread(mine.astype(jnp.bfloat16), replicas), ALL)
    update, right, new_errors = finish(right, ortho, merged, replicas)
    return update, right.T, new_errors[None]


def solution(mesh):
    chips = Mesh(mesh.devices.reshape(4, 4, 2, 8), ("y", "x", "core", "z"))
    placed = (P(DP, None, "z"), P(DP, None, "z"), P("z", None))
    return jax.shard_map(
        per_device,
        mesh=chips,
        in_specs=placed,
        out_specs=(P(DP, "z"), P("z", None), P(DP, None, "z")),
        check_vma=False,
    )
```
